128 devices in a mesh: dp: 16 (over z, y), expert: 8 (over x, core).
Axes of the slice: x: 4, y: 4, z: 4, core: 2. Of those that a mesh axis runs over, the one named last changes fastest.
Arguments:
- tokens: bfloat16 [32768, 768], P(('dp', 'expert')), may hold values from -6 to 6
- w_qkv: bfloat16 [768, 2304], P(('dp', 'expert')), may hold values from -0.21875 to 0.21875
- w_attn_out: bfloat16 [768, 768], P(('dp', 'expert')), may hold values from -1.25 to 1.25
- w_router: bfloat16 [768, 8], P(('dp', 'expert')), may hold values from -0.15625 to 0.15625
- gain_attn: bfloat16 [768], P(('dp', 'expert')), may hold values from 0.5 to 1.5
- gain_moe: bfloat16 [768], P(('dp', 'expert')), may hold values from 0.5 to 1.5
- bias_table: bfloat16 [384], P(('dp', 'expert')), may hold values from -4 to 4
- w_in: bfloat16 [8, 3072, 768], P('expert', 'dp'), may hold values from -0.21875 to 0.21875
- w_out: bfloat16 [8, 3072, 768], P('expert', 'dp'), may hold values from -1.25 to 1.25
- expert_ids: int32 [32768], P(('dp', 'expert')), may hold values from 0 to 7, as said below
- slots: int32 [32768], P(('dp', 'expert')), may hold values from 0 to 16, as said below
- buckets: int32 [128, 128], replicated, may hold values from 0 to 31
- cotangent: float32 [32768, 768], P(('dp', 'expert')), may hold values from -6 to 6
Outputs:
- output: float32 [32768, 768], P(('dp', 'expert'))
- grad_tokens: float32 [32768, 768], P(('dp', 'expert'))
- grad_qkv: float32 [768, 2304], P(('dp', 'expert'))
- grad_attn_out: float32 [768, 768], P(('dp', 'expert'))
- grad_router: float32 [768, 8], P(('dp', 'expert'))
- grad_gain_attn: float32 [768], P(('dp', 'expert'))
- grad_gain_moe: float32 [768], P(('dp', 'expert'))
- grad_bias: float32 [384], P(('dp', 'expert'))
- grad_in: float32 [8, 3072, 768], P('expert', 'dp')
- grad_out: float32 [8, 3072, 768], P('expert', 'dp')
The draws below stay inside these ranges and needn't reach their ends.
Inputs may be any that keep to these rules, and one draw needn't show every extreme that they name: `expert_ids`: every number names an expert; tokens of one sequence are one block of 128 rows. slots[t] is the number of earlier tokens of t's sequence that name the same expert as t, capped at 16; the value 16 marks a token that its expert drops.
All inputs are finite; a program needn't handle non-finite values.
Results may differ from the reference program's by a relative error of at most 0.029.
Values may be sent and summed in bfloat16 or wider, within the bound.
A program may use at most 192 MiB of HBM per device.

```python
import math
import jax
import jax.numpy as jnp
from jax import lax

MODEL_WIDTH = 768
HEADS = 12
HEAD_DIM = 64
FF = 3072
BUCKETS = 32
LEN = 128
MICRO = 2
EXPERT_COUNT = 8
TOKENS = 32768


def routing_draw(key):
    base_key = jax.random.fold_in(key, 17)
    key_hot, key_base, key_pick = jax.random.split(base_key, 3)
    seq_count = TOKENS // LEN
    seq_index = jnp.arange(seq_count, dtype=jnp.int32)
    group_index = seq_index // (MICRO * EXPERT_COUNT) * MICRO + seq_index % MICRO
    hot_table = jax.random.randint(key_hot, (seq_count,), 0, EXPERT_COUNT, dtype=jnp.int32)
    hot_expert = hot_table[group_index]
    base_ids = jax.random.randint(key_base, (seq_count, LEN), 0, EXPERT_COUNT, dtype=jnp.int32)
    positions = jnp.arange(LEN, dtype=jnp.int32)
    order_keys = jax.random.randint(key_pick, (seq_count, LEN), 0, LEN, dtype=jnp.int32) * LEN + positions[None]
    ranks = jnp.argsort(jnp.argsort(order_keys, axis=1), axis=1)
    forced = ranks < LEN // 4
    route_ids = jnp.where(forced, hot_expert[:, None], base_ids).astype(jnp.int32)
    onehot = (route_ids[:, :, None] == jnp.arange(EXPERT_COUNT, dtype=jnp.int32)[None, None]).astype(jnp.int32)
    running = jnp.cumsum(onehot, axis=1) - 1
    slot_ids = jnp.minimum(jnp.sum(running * onehot, axis=2), LEN // EXPERT_COUNT).astype(jnp.int32)
    return (route_ids.reshape(-1), slot_ids.reshape(-1))


def draw_expert_ids(key, part):
    return routing_draw(key)[0]


def draw_slots(key, part):
    return routing_draw(key)[1]


def place_ends(entries, key, low, largest):
    shape = entries.shape
    index_at = [jax.random.randint(jax.random.fold_in(key, axis), (), 0, shape[axis]) for axis in range(len(shape))]
    entries = entries.at[tuple(index_at)].set(low)
    longest = shape.index(max(shape))
    index_at[longest] = (index_at[longest] + 1) % shape[longest]
    return entries.at[tuple(index_at)].set(largest)


def level_of(stream_key, dims, pieces, low, largest):
    factor_of = 1.0
    for position, blocks in pieces:
        draws = jax.random.uniform(jax.random.fold_in(jax.random.fold_in(stream_key, 6), position), (blocks,), jnp.float32, low / len(pieces), largest / len(pieces))
        factor_of = factor_of * jnp.repeat(jnp.exp(draws), dims[position] // blocks).reshape((-1,) + (1,) * (len(dims) - 1 - position))
    return factor_of


def gaussian(stream_key, dims, scale, limit, cuts=(), held_as=jnp.bfloat16):
    drawn = jax.random.normal(stream_key, dims, jnp.float32) * scale
    if len(cuts) > 0:
        drawn = level_of(stream_key, dims, cuts, -0.22, 0.18) * drawn
    return jnp.clip(drawn, min=-limit, max=limit).astype(held_as)


def setup_inputs(seed: int = 0) -> dict:
    key_of = jax.random.split(jax.random.key(seed), 14)
    return {
        "tokens": gaussian(key_of[0], (TOKENS, MODEL_WIDTH), 1.0, 6.0, ((0, 128),)),
        "w_qkv": gaussian(key_of[1], (MODEL_WIDTH, 3 * MODEL_WIDTH), MODEL_WIDTH ** -0.5, 0.21875, ((0, 128),)),
        "w_attn_out": gaussian(key_of[2], (MODEL_WIDTH, MODEL_WIDTH), (MODEL_WIDTH // 32) ** -0.5, 1.25, ((0, 128),)),
        "w_router": gaussian(key_of[3], (MODEL_WIDTH, EXPERT_COUNT), (2 * MODEL_WIDTH) ** -0.5, 0.15625, ((0, 128),)),
        "gain_attn": jnp.clip(1.0 + 0.1 * jax.random.normal(key_of[4], (MODEL_WIDTH,), jnp.float32), 0.5, 1.5).astype(jnp.bfloat16),
        "gain_moe": jnp.clip(1.0 + 0.1 * jax.random.normal(key_of[5], (MODEL_WIDTH,), jnp.float32), 0.5, 1.5).astype(jnp.bfloat16),
        "bias_table": gaussian(key_of[6], (BUCKETS * HEADS,), 1.0, 4.0, ((0, 128),)),
        "w_in": gaussian(key_of[7], (EXPERT_COUNT, FF, MODEL_WIDTH), MODEL_WIDTH ** -0.5, 0.21875, ((0, 8), (1, 16))),
        "w_out": gaussian(key_of[8], (EXPERT_COUNT, FF, MODEL_WIDTH), (max(FF // 128, 1)) ** -0.5, 1.25, ((0, 8), (1, 16))),
        "expert_ids": draw_expert_ids(jax.random.fold_in(key_of[13], 71), 0),
        "slots": draw_slots(jax.random.fold_in(key_of[13], 71), 0),
        "buckets": place_ends(jax.random.randint(key_of[11], (LEN, LEN), 0, BUCKETS), jax.random.fold_in(key_of[11], 1), 0, BUCKETS - 1).astype(jnp.int32),
        "cotangent": gaussian(key_of[12], (TOKENS, MODEL_WIDTH), 1.0, 6.0, ((0, 128),), jnp.float32),
    }


NORM_EPS = 1e-06
HIGH_PRECISION = lax.Precision.HIGHEST

@jax.custom_vjp
def low_precision(v):
    return lax.optimization_barrier(v.astype(jnp.bfloat16)).astype(jnp.float32)

@jax.custom_vjp
def low_precision_back(v):
    return v

def low_keep(v):
    return (low_precision(v), None)

def low_pass(kept, grad):
    return (grad,)

def back_keep(v):
    return (v, None)

def back_low(kept, grad):
    return (low_precision(grad),)
low_precision.defvjp(low_keep, low_pass)
low_precision_back.defvjp(back_keep, back_low)

def rms_scale(values, gain):
    return values * lax.rsqrt(lax.optimization_barrier(jnp.mean(values * values, axis=-1, keepdims=True)) + NORM_EPS) * gain

def reference(tokens, w_qkv, w_attn_out, w_router, gain_attn, gain_moe, bias_table, w_in, w_out, expert_ids, slots, buckets, cotangent):
    expert_capacity = LEN // EXPERT_COUNT
    seq_count = TOKENS // LEN
    group = math.gcd(seq_count, 32)
    block_count = seq_count // group
    route_blocks = expert_ids.reshape(block_count, group, LEN)
    slot_blocks = slots.reshape(block_count, group, LEN)
    levels = lax.broadcasted_iota(jnp.int32, (BUCKETS, LEN, LEN), 0)
    bucket_onehot = (levels == buckets[None]).astype(jnp.float32)
    floats = tuple((a.astype(jnp.float32) for a in (tokens, w_qkv, w_attn_out, w_router, gain_attn, gain_moe, bias_table, w_in, w_out)))

    def forward(x_all, query_key_value_weight, attention_out_weight, router_weight, gain_one, gain_two, bias_flat, win, wout):
        full_bias = jnp.einsum('bij,bh->hij', bucket_onehot, bias_flat.reshape(BUCKETS, HEADS), precision=HIGH_PRECISION)

        def one_block(blocks):
            input_rows, route_ids, slot_ids = blocks
            token_group_size = input_rows.shape[0]
            first_normed = low_precision(rms_scale(input_rows, gain_one))
            query_key_value_rows = low_precision(low_precision_back(jnp.einsum('tog,gz->toz', first_normed, query_key_value_weight, precision=HIGH_PRECISION)))
            parts = query_key_value_rows.reshape(token_group_size, LEN, 3, HEADS, HEAD_DIM)
            queries, key_rows, value_rows = (parts[:, :, 0], parts[:, :, 1], parts[:, :, 2])
            raw = low_precision_back(jnp.einsum('sihc,sjhc->shij', queries, key_rows, precision=HIGH_PRECISION) * HEAD_DIM ** (-0.5))
            attn_probs = jax.nn.softmax(raw + full_bias[None], axis=-1)
            mixed_output = jnp.einsum('shij,sjhc->sihc', low_precision(attn_probs), value_rows, precision=HIGH_PRECISION).reshape(token_group_size, LEN, MODEL_WIDTH)
            mixed_output = low_precision(low_precision_back(mixed_output))
            residual_stream = input_rows + low_precision_back(jnp.einsum('tog,gz->toz', mixed_output, attention_out_weight, precision=HIGH_PRECISION))
            second_normed = low_precision(rms_scale(residual_stream, gain_two))
            router_logits = jnp.einsum('tog,gz->toz', second_normed, router_weight, precision=HIGH_PRECISION)
            onehot = (route_ids[..., None] == jnp.arange(EXPERT_COUNT, dtype=jnp.int32)).astype(jnp.float32)
            gate = lax.optimization_barrier(jnp.sum(jax.nn.softmax(router_logits, axis=-1) * onehot, axis=-1))
            target = route_ids * expert_capacity + slot_ids
            columns = jnp.arange(EXPERT_COUNT * expert_capacity, dtype=jnp.int32)
            routing_table = ((target[..., None] == columns) & (slot_ids[..., None] < expert_capacity)).astype(jnp.float32)
            sent_tokens = jnp.einsum('tib,tij->tbj', routing_table, low_precision_back(second_normed), precision=HIGH_PRECISION).reshape(token_group_size, EXPERT_COUNT, expert_capacity, MODEL_WIDTH)
            pre_act = low_precision_back(jnp.einsum('secd,efd->secf', sent_tokens, win, precision=HIGH_PRECISION))
            hidden_low = low_precision(jax.nn.gelu(pre_act))
            layer_result = low_precision(low_precision_back(jnp.einsum('secf,efd->secd', hidden_low, wout, precision=HIGH_PRECISION)))
            layer_result = layer_result.reshape(token_group_size, EXPERT_COUNT * expert_capacity, MODEL_WIDTH)
            combined_output = jnp.einsum('thx,txw->thw', routing_table, layer_result, precision=HIGH_PRECISION)
            return residual_stream + gate[..., None] * combined_output
        outputs = lax.map(jax.checkpoint(one_block), (x_all.reshape(block_count, group, LEN, MODEL_WIDTH), route_blocks, slot_blocks))
        return outputs.reshape(TOKENS, MODEL_WIDTH)
    output, pullback = jax.vjp(forward, *floats)
    grads = pullback(cotangent)
    return (output, grads[0], grads[1], grads[2], grads[3], grads[4], grads[5], grads[6], grads[7], grads[8])
```

```python
import functools

import jax
import jax.numpy as jnp
import numpy as np
from jax import lax
from jax.experimental import pallas as pl
from jax.experimental.pallas import tpu as pltpu
from jax.sharding import PartitionSpec as P

MESH = pl.DeviceIdType.MESH
HEADS = 12
HEAD_DIM = 64
BUCKETS = 32
LEN = 128
WIDTH = 768
FF = 3072
EXPERTS = 8
DP = 16
CAP = 16
SHARD = FF // DP
COLS = 384
ROWS = 48
NORM_EPS = 1e-06
HIGH = lax.Precision.HIGHEST
F32 = jnp.float32
BF16 = jnp.bfloat16
MIB = 1 << 20


def place_matrix():
    m = np.zeros((160, 384), np.float32)
    for c in range(3):
        for e in range(8):
            for r in range(6):
                m[c * 48 + e * 6 + r, e * 48 + c * 6 + r] = 1
    for e in range(8):
        m[144 + e, e * 48 + 32] = 1
    return m


def spread_matrix():
    m = np.zeros((256, 144), np.float32)
    for c in range(3):
        for e in range(8):
            for r in range(6):
                m[e * 32 + c * 6 + r, c * 48 + e * 6 + r] = 1
    return m


class Where:
    def __init__(self):
        self.dp = lax.axis_index("dp")
        self.e = lax.axis_index("expert")
        self.z, self.y = lax.div(self.dp, 4), lax.rem(self.dp, 4)
        self.x, self.c = lax.div(self.e, 2), lax.rem(self.e, 2)
        self.partner_e = self.x * 2 + (1 - self.c)
        self.partner = {"expert": self.partner_e}

    def at(self, axis, step):
        if axis == "y":
            return self.z * 4 + lax.rem(self.y + step + 4, 4)
        if axis == "z":
            return lax.rem(self.z + step + 4, 4) * 4 + self.y
        return lax.rem(self.x + step + 4, 4) * 2 + self.c

    def dev(self, axis, step):
        return {"expert" if axis == "x" else "dp": self.at(axis, step)}

    def at2(self, axis1, step1, step2):
        dy, dz = (step1, step2) if axis1 == "y" else (step2, step1)
        return lax.rem(self.z + dz + 4, 4) * 4 + lax.rem(self.y + dy + 4, 4)


def greet(w, dp_too):
    barrier = pltpu.get_barrier_semaphore()

    def hello_e(k, n):
        pl.semaphore_signal(
            barrier, inc=1, device_id={"expert": lax.rem(w.e + k, EXPERTS)}, device_id_type=MESH
        )
        return n

    def hello_dp(k, n):
        pl.semaphore_signal(
            barrier, inc=1, device_id={"dp": lax.rem(w.dp + k, DP)}, device_id_type=MESH
        )
        return n

    lax.fori_loop(1, EXPERTS, hello_e, 0)
    if dp_too:
        lax.fori_loop(1, DP, hello_dp, 0)
    pl.semaphore_wait(barrier, EXPERTS - 1 + (DP - 1 if dp_too else 0))


def remote(src, dst, send, recv, dev):
    return pltpu.make_async_remote_copy(
        src_ref=src, dst_ref=dst, send_sem=send, recv_sem=recv, device_id=dev, device_id_type=MESH
    )


class RingGather:
    def __init__(self, w, axis, place, rows, send, recv, base, own=None):
        self.w, self.axis, self.place, self.half = w, axis, place, rows // 2
        self.send, self.recv, self.base = send, recv, base
        self.own = place(0) if own is None else own
        self.copies = []

    def _go(self, k, src, dst, step):
        copy = remote(
            src,
            dst,
            self.send.at[self.base + k],
            self.recv.at[self.base + k],
            self.w.dev(self.axis, step),
        )
        copy.start()
        self.copies.append(copy)

    def start(self):
        self._go(0, self.own, self.place(0), 1)
        self._go(1, self.own, self.place(0), -1)

    def relay(self):
        h = self.half
        self.copies[0].wait_recv()
        low = self.place(-1).at[pl.ds(0, h)]
        self._go(2, low, low, 1)
        self.copies[1].wait_recv()
        high = self.place(1).at[pl.ds(h, h)]
        self._go(3, high, high, -1)

    def finish(self):
        self.copies[2].wait_recv()
        self.copies[3].wait_recv()

    def drain(self):
        for copy in self.copies:
            copy.wait_send()


def gather_kernel(
    win_ref,
    wout_ref,
    first_ref,
    place_ref,
    in_ref,
    out_ref,
    dense_ref,
    extra_ref,
    got,
    piece,
    extra_piece,
    own_sem,
    a2a_send,
    a2a_recv,
    dp_send,
    dp_recv,
    ring_send,
    ring_recv,
    x_send,
    x_recv,
):
    w = Where()
    greet(w, True)

    def to_expert(k):
        peer = lax.rem(w.e + k, EXPERTS)
        return remote(
            first_ref.at[peer], got.at[w.e], a2a_send.at[k], a2a_recv.at[k], {"expert": peer}
        )

    def start_a2a(k, n):
        to_expert(k).start()
        return n

    lax.fori_loop(1, EXPERTS, start_a2a, 0)
    got[w.e] = first_ref[w.e]

    keep_in = pltpu.make_async_copy(win_ref, in_ref.at[w.dp], own_sem.at[0])
    keep_out = pltpu.make_async_copy(wout_ref, out_ref.at[w.dp], own_sem.at[1])
    keep_in.start()
    keep_out.start()
    one, two = {}, {}
    for n, (ref, own, axis1, axis2) in enumerate(
        ((in_ref, win_ref, "y", "z"), (out_ref, wout_ref, "z", "y"))
    ):
        one[n] = RingGather(
            w,
            axis1,
            lambda s, ref=ref, a=axis1: ref.at[w.at2(a, s, 0)],
            SHARD,
            ring_send,
            ring_recv,
            n * 20,
            own=own,
        )
        for k, o in enumerate((0, -1, 1, 2)):
            two[n, o] = RingGather(
                w,
                axis2,
                lambda s, ref=ref, a=axis1, o=o: ref.at[w.at2(a, o, s)],
                SHARD,
                ring_send,
                ring_recv,
                n * 20 + 4 + 4 * k,
                own=own if o == 0 else None,
            )
    for n in range(2):
        one[n].start()
    for n in range(2):
        two[n, 0].start()

    def end_a2a(k, n):
        copy = to_expert(k)
        copy.wait_recv()
        copy.wait_send()
        return n

    lax.fori_loop(1, EXPERTS, end_a2a, 0)
    placed = jnp.dot(place_ref[...], got[...].reshape(384, 128), preferred_element_type=F32).astype(
        BF16
    )
    for c in range(3):
        piece[:, c * 128 : (c + 1) * 128] = placed[c * 48 : (c + 1) * 48]
    extra_piece[...] = placed[144:160]
    mine = pl.ds(pl.multiple_of(w.dp * ROWS, 16), ROWS)
    keep_piece = pltpu.make_async_copy(piece, dense_ref.at[w.e, mine], own_sem.at[2])
    keep_extra = pltpu.make_async_copy(extra_piece, extra_ref.at[w.dp], own_sem.at[3])
    keep_piece.start()
    keep_extra.start()

    def to_dp(k):
        dev = {"dp": lax.rem(w.dp + k, DP)}
        return (
            remote(piece, dense_ref.at[w.e, mine], dp_send.at[0, k], dp_recv.at[0, k], dev),
            remote(extra_piece, extra_ref.at[w.dp], dp_send.at[1, k], dp_recv.at[1, k], dev),
        )

    def start_dp(k, n):
        for copy in to_dp(k):
            copy.start()
        return n

    def end_dp(k, n):
        for copy in to_dp(k):
            copy.wait_recv()
            copy.wait_send()
        return n

    lax.fori_loop(1, DP, start_dp, 0)
    for n in range(2):
        one[n].relay()
        two[n, -1].start()
        two[n, 1].start()
    lax.fori_loop(1, DP, end_dp, 0)
    keep_piece.wait()
    ring = RingGather(w, "x", lambda s: dense_ref.at[w.at("x", s)], WIDTH, x_send, x_recv, 0)
    ring.start()

    def across(k, ref):
        copy = remote(ref, ref, x_send.at[4 + k], x_recv.at[4 + k], w.partner)
        copy.start()
        return copy

    pair = [across(0, dense_ref.at[w.e])]
    for n in range(2):
        two[n, 0].relay()
    for n in range(2):
        one[n].finish()
        two[n, 2].start()
    ring.relay()
    pair.append(across(1, dense_ref.at[w.at("x", -1)]))
    pair.append(across(2, dense_ref.at[w.at("x", 1)]))
    for n in range(2):
        two[n, -1].relay()
        two[n, 1].relay()
    ring.finish()
    pair.append(across(3, dense_ref.at[w.at("x", 2)]))
    for n in range(2):
        two[n, 2].relay()
    for n in range(2):
        for o in (0, -1, 1, 2):
            two[n, o].finish()
    for copy in pair:
        copy.wait_recv()
        copy.wait_send()
    ring.drain()
    for n in range(2):
        one[n].drain()
        for o in (0, -1, 1, 2):
            two[n, o].drain()
    keep_in.wait()
    keep_out.wait()
    keep_extra.wait()


def gather(win, wout, first):
    hbm = pl.BlockSpec(memory_space=pl.ANY)
    vmem = pl.BlockSpec(memory_space=pltpu.VMEM)
    return pl.pallas_call(
        gather_kernel,
        out_shape=(
            jax.ShapeDtypeStruct((DP, SHARD, WIDTH), BF16),
            jax.ShapeDtypeStruct((DP, SHARD, WIDTH), BF16),
            jax.ShapeDtypeStruct((EXPERTS, WIDTH, COLS), BF16),
            jax.ShapeDtypeStruct((DP, 16, 128), BF16),
        ),
        in_specs=[hbm, hbm, vmem, vmem],
        out_specs=(hbm, hbm, hbm, hbm),
        scratch_shapes=[
            pltpu.VMEM((EXPERTS, 48, 128), BF16),
            pltpu.VMEM((ROWS, COLS), BF16),
            pltpu.VMEM((16, 128), BF16),
            pltpu.SemaphoreType.DMA((4,)),
            pltpu.SemaphoreType.DMA((EXPERTS,)),
            pltpu.SemaphoreType.DMA((EXPERTS,)),
            pltpu.SemaphoreType.DMA((2, DP)),
            pltpu.SemaphoreType.DMA((2, DP)),
            pltpu.SemaphoreType.DMA((40,)),
            pltpu.SemaphoreType.DMA((40,)),
            pltpu.SemaphoreType.DMA((8,)),
            pltpu.SemaphoreType.DMA((8,)),
        ],
        compiler_params=pltpu.CompilerParams(
            collective_id=0, has_side_effects=True, vmem_limit_bytes=32 * MIB
        ),
        name="gather_weights",
    )(win, wout, first, jnp.asarray(place_matrix(), BF16))


def exchange_kernel(src_ref, dst_ref, own_sem, send, recv):
    w = Where()
    greet(w, False)

    def to(k):
        peer = lax.rem(w.e + k, EXPERTS)
        return remote(src_ref.at[peer], dst_ref.at[w.e], send.at[k], recv.at[k], {"expert": peer})

    def begin(k, n):
        to(k).start()
        return n

    def end(k, n):
        copy = to(k)
        copy.wait_recv()
        copy.wait_send()
        return n

    lax.fori_loop(1, EXPERTS, begin, 0)
    keep = pltpu.make_async_copy(src_ref.at[w.e], dst_ref.at[w.e], own_sem)
    keep.start()
    lax.fori_loop(1, EXPERTS, end, 0)
    keep.wait()


def exchange(blocks, number, name):
    hbm = pl.BlockSpec(memory_space=pl.ANY)
    return pl.pallas_call(
        exchange_kernel,
        out_shape=jax.ShapeDtypeStruct(blocks.shape, blocks.dtype),
        in_specs=[hbm],
        out_specs=hbm,
        scratch_shapes=[
            pltpu.SemaphoreType.DMA,
            pltpu.SemaphoreType.DMA((EXPERTS,)),
            pltpu.SemaphoreType.DMA((EXPERTS,)),
        ],
        compiler_params=pltpu.CompilerParams(collective_id=number, has_side_effects=True),
        name=name,
    )(blocks)


def add_rows(rows, step, dst, *srcs):
    def body(i, n):
        part = pl.ds(pl.multiple_of(i * step, step), step)
        total = srcs[0][part].astype(F32)
        for src in srcs[1:]:
            total = total + src[part].astype(F32)
        dst[part] = total.astype(dst.dtype)
        return n

    lax.fori_loop(0, rows // step, body, 0)


class RingSum:
    def __init__(self, w, axis, place, rows, relayed, landed, send, recv, base):
        self.w, self.axis, self.place, self.rows, self.half = w, axis, place, rows, rows // 2
        self.relayed, self.landed = relayed, landed
        self.send, self.recv, self.base = send, recv, base
        self.copies = {}

    def _go(self, k, src, dst, step):
        copy = remote(
            src,
            dst,
            self.send.at[self.base + k],
            self.recv.at[self.base + k],
            self.w.dev(self.axis, step),
        )
        copy.start()
        self.copies[k] = copy

    def _part(self, ref, k):
        return ref.at[pl.ds(k * self.half, self.half)]

    def far(self):
        self._go(0, self._part(self.place(2), 0), self.relayed.at[0], 1)
        self._go(1, self._part(self.place(2), 1), self.relayed.at[1], -1)

    def near(self):
        self._go(2, self._part(self.place(1), 1), self._part(self.landed.at[0], 1), 1)
        self._go(3, self._part(self.place(-1), 0), self._part(self.landed.at[1], 0), -1)

    def relay(self):
        self.copies[0].wait_recv()
        low = self._part(self.place(1), 0)
        add_rows(self.half, 32, low, low, self.relayed.at[0])
        self._go(4, low, self._part(self.landed.at[0], 0), 1)
        self.copies[1].wait_recv()
        high = self._part(self.place(-1), 1)
        add_rows(self.half, 32, high, high, self.relayed.at[1])
        self._go(5, high, self._part(self.landed.at[1], 1), -1)

    def finish(self, dst):
        for k in (2, 3, 4, 5):
            self.copies[k].wait_recv()
        add_rows(self.rows, 32, dst, self.place(0), self.landed.at[0], self.landed.at[1])

    def drain(self):
        for k in range(6):
            self.copies[k].wait_send()


def reduce_kernel(
    gin_ref,
    gout_ref,
    dense_ref,
    extra_ref,
    spread_ref,
    in_ref,
    out_ref,
    dense_out_ref,
    extra_out_ref,
    grads,
    relayed,
    landed,
    dense,
    crossed,
    x_relayed,
    x_landed,
    dp_got,
    dp_extra,
    extra_sum,
    last,
    last_got,
    extra_got,
    own_sem,
    ring_send,
    ring_recv,
    x_send,
    x_recv,
    dp_send,
    dp_recv,
    a2a_send,
    a2a_recv,
):
    w = Where()
    load_in = pltpu.make_async_copy(gin_ref, grads.at[0], own_sem.at[0])
    load_out = pltpu.make_async_copy(gout_ref, grads.at[1], own_sem.at[1])
    load_dense = pltpu.make_async_copy(dense_ref, dense, own_sem.at[2])
    load_in.start()
    load_out.start()
    load_dense.start()
    greet(w, True)
    axes = (("y", "z"), ("z", "y"))
    order = (2, 1, -1, 0)
    one, two = {}, {}
    for n, (axis1, axis2) in enumerate(axes):
        for k, o in enumerate(order):
            two[n, o] = RingSum(
                w,
                axis2,
                lambda s, n=n, a=axis1, o=o: grads.at[n, w.at2(a, o, s)],
                SHARD,
                relayed.at[n * 5 + k],
                landed.at[n * 5 + k],
                ring_send,
                ring_recv,
                (n * 5 + k) * 6,
            )
        one[n] = RingSum(
            w,
            axis1,
            lambda s, n=n, a=axis1: grads.at[n, w.at2(a, s, 0)],
            SHARD,
            relayed.at[n * 5 + 4],
            landed.at[n * 5 + 4],
            ring_send,
            ring_recv,
            (n * 5 + 4) * 6,
        )
    load_in.wait()
    load_out.wait()
    for n in range(2):
        two[n, 2].far()
    for n in range(2):
        for o in (1, -1, 0):
            two[n, o].far()
    for n in range(2):
        two[n, 2].near()
    for n in range(2):
        for o in (1, -1, 0):
            two[n, o].near()
    load_dense.wait()
    pair = []
    for k in range(4):
        copy = remote(
            dense.at[2 * k + 1 - w.c],
            crossed.at[k],
            x_send.at[6 + k],
            x_recv.at[6 + k],
            w.partner,
        )
        copy.start()
        pair.append(copy)

    def extra_dp(k):
        peer = lax.rem(w.dp + k, DP)
        return remote(
            extra_ref.at[peer], dp_extra.at[w.dp], dp_send.at[1, k], dp_recv.at[1, k], {"dp": peer}
        )

    def start_extra(k, n):
        extra_dp(k).start()
        return n

    lax.fori_loop(1, DP, start_extra, 0)
    dp_extra[w.dp] = extra_ref[w.dp]
    for n in range(2):
        two[n, 2].relay()
    for k in range(4):
        pair[k].wait_recv()
        add_rows(WIDTH, 32, dense.at[2 * k + w.c], dense.at[2 * k + w.c], crossed.at[k])
    ring = RingSum(
        w, "x", lambda s: dense.at[w.at("x", s)], WIDTH, x_relayed, x_landed, x_send, x_recv, 0
    )
    ring.far()
    ring.near()
    for o in (1, -1, 0):
        for n in range(2):
            two[n, o].relay()
    ring.relay()
    for n in range(2):
        two[n, 2].finish(grads.at[n, w.at2(axes[n][0], 2, 0)])
        one[n].far()
    for n in range(2):
        for o in (1, -1):
            two[n, o].finish(grads.at[n, w.at2(axes[n][0], o, 0)])
        one[n].near()
    for n in range(2):
        one[n].relay()
        two[n, 0].finish(grads.at[n, w.dp])
    ring.finish(dense.at[w.e])

    def rows_of(dp):
        return pl.ds(pl.multiple_of(dp * ROWS, 16), ROWS)

    def dense_dp(k):
        peer = lax.rem(w.dp + k, DP)
        return remote(
            dense.at[w.e, rows_of(peer)],
            dp_got.at[w.dp],
            dp_send.at[0, k],
            dp_recv.at[0, k],
            {"dp": peer},
        )

    def start_dp(k, n):
        dense_dp(k).start()
        return n

    def end_dp(k, n):
        for copy in (dense_dp(k), extra_dp(k)):
            copy.wait_recv()
            copy.wait_send()
        return n

    lax.fori_loop(1, DP, start_dp, 0)
    dp_got[w.dp] = dense[w.e, rows_of(w.dp)]
    for n, ref in ((0, in_ref), (1, out_ref)):
        one[n].finish(ref)
    lax.fori_loop(1, DP, end_dp, 0)
    total = dp_got[0].astype(F32)
    extra_total = dp_extra[0]
    for k in range(1, DP):
        total = total + dp_got[k].astype(F32)
        extra_total = extra_total + dp_extra[k]
    extra_sum[...] = extra_total
    flat = jnp.concatenate([total[:, c * 128 : (c + 1) * 128] for c in range(3)], axis=0)
    last[...] = (
        jnp.dot(spread_ref[...], flat.astype(BF16), preferred_element_type=F32)
        .astype(BF16)
        .reshape(EXPERTS, 32, 128)
    )

    def to_expert(k):
        peer = lax.rem(w.e + k, EXPERTS)
        dev = {"expert": peer}
        return (
            remote(last.at[peer], last_got.at[w.e], a2a_send.at[0, k], a2a_recv.at[0, k], dev),
            remote(extra_sum, extra_got.at[w.e], a2a_send.at[1, k], a2a_recv.at[1, k], dev),
        )

    def start_a2a(k, n):
        for copy in to_expert(k):
            copy.start()
        return n

    def end_a2a(k, n):
        for copy in to_expert(k):
            copy.wait_recv()
            copy.wait_send()
        return n

    lax.fori_loop(1, EXPERTS, start_a2a, 0)
    last_got[w.e] = last[w.e]
    extra_got[w.e] = extra_sum[...]
    lax.fori_loop(1, EXPERTS, end_a2a, 0)
    dense_out_ref[...] = last_got[...].astype(F32)
    extra_total = extra_got[0]
    for k in range(1, EXPERTS):
        extra_total = extra_total + extra_got[k]
    extra_out_ref[...] = extra_total
    for copy in pair:
        copy.wait_send()
    ring.drain()
    for n in range(2):
        one[n].drain()
        for o in order:
            two[n, o].drain()


def reduce(gin, gout, dense, extra):
    hbm = pl.BlockSpec(memory_space=pl.ANY)
    vmem = pl.BlockSpec(memory_space=pltpu.VMEM)
    half = SHARD // 2
    return pl.pallas_call(
        reduce_kernel,
        out_shape=(
            jax.ShapeDtypeStruct((SHARD, WIDTH), F32),
            jax.ShapeDtypeStruct((SHARD, WIDTH), F32),
            jax.ShapeDtypeStruct((EXPERTS, 32, 128), F32),
            jax.ShapeDtypeStruct((16, 128), F32),
        ),
        in_specs=[hbm, hbm, hbm, vmem, vmem],
        out_specs=(vmem, vmem, vmem, vmem),
        scratch_shapes=[
            pltpu.VMEM((2, DP, SHARD, WIDTH), BF16),
            pltpu.VMEM((10, 2, half, WIDTH), BF16),
            pltpu.VMEM((10, 2, SHARD, WIDTH), BF16),
            pltpu.VMEM((EXPERTS, WIDTH, COLS), BF16),
            pltpu.VMEM((4, WIDTH, COLS), BF16),
            pltpu.VMEM((2, WIDTH // 2, COLS), BF16),
            pltpu.VMEM((2, WIDTH, COLS), BF16),
            pltpu.VMEM((DP, ROWS, COLS), BF16),
            pltpu.VMEM((DP, 16, 128), F32),
            pltpu.VMEM((16, 128), F32),
            pltpu.VMEM((EXPERTS, 32, 128), BF16),
            pltpu.VMEM((EXPERTS, 32, 128), BF16),
            pltpu.VMEM((EXPERTS, 16, 128), F32),
            pltpu.SemaphoreType.DMA((3,)),
            pltpu.SemaphoreType.DMA((60,)),
            pltpu.SemaphoreType.DMA((60,)),
            pltpu.SemaphoreType.DMA((10,)),
            pltpu.SemaphoreType.DMA((10,)),
            pltpu.SemaphoreType.DMA((2, DP)),
            pltpu.SemaphoreType.DMA((2, DP)),
            pltpu.SemaphoreType.DMA((2, EXPERTS)),
            pltpu.SemaphoreType.DMA((2, EXPERTS)),
        ],
        compiler_params=pltpu.CompilerParams(
            collective_id=1, has_side_effects=True, vmem_limit_bytes=56 * MIB
        ),
        name="reduce_gradients",
    )(gin, gout, dense, extra, jnp.asarray(spread_matrix(), BF16))


def contract_last(left, right):
    return lax.dot_general(left, right, (((1,), (1,)), ((), ())), preferred_element_type=F32)


def contract_first(left, right):
    return lax.dot_general(left, right, (((0,), (0,)), ((), ())), preferred_element_type=F32)


def local(
    tokens,
    w_qkv,
    w_attn_out,
    w_router,
    gain_attn,
    gain_moe,
    bias_table,
    w_in,
    w_out,
    expert_ids,
    slots,
    buckets,
    cotangent,
):
    seqs = tokens.shape[0] // LEN
    scale = HEAD_DIM ** (-0.5)
    me = lax.axis_index("expert")

    dense = jnp.concatenate([w_qkv, w_attn_out], axis=1)
    first = dense.reshape(6, EXPERTS, 3, 128).transpose(1, 2, 0, 3).reshape(EXPERTS, 18, 128)
    small = jnp.concatenate([w_router.reshape(48), gain_attn, gain_moe, bias_table])
    small = jnp.broadcast_to(jnp.pad(small, (0, 65))[None, None], (EXPERTS, 1, 128))
    first = jnp.concatenate(
        [first, jnp.zeros((EXPERTS, 14, 128), BF16), small, jnp.zeros((EXPERTS, 15, 128), BF16)],
        axis=1,
    )
    all_in, all_out, dense, extra = gather(w_in[0], w_out[0], first)
    all_in = all_in.reshape(FF, WIDTH)
    all_out = all_out.reshape(FF, WIDTH)
    wqkv = dense[:6].transpose(1, 0, 2).reshape(WIDTH, 3 * WIDTH)
    wattn = dense[6:].transpose(1, 0, 2).reshape(WIDTH, WIDTH)
    extra = extra[:, :8].reshape(128, 128).astype(F32)
    router = extra[:, :48].reshape(WIDTH, EXPERTS)
    gain_one = extra[:, 48:54].reshape(WIDTH)
    gain_two = extra[:, 54:60].reshape(WIDTH)
    table = extra[:, 60:63].reshape(BUCKETS, HEADS)

    levels = lax.broadcasted_iota(jnp.int32, (BUCKETS, LEN, LEN), 0)
    bucket_onehot = (levels == buckets[None]).astype(F32)
    full_bias = jnp.einsum("bij,bh->hij", bucket_onehot, table, precision=HIGH)

    x = tokens.astype(F32)
    rho1 = lax.rsqrt(jnp.mean(x * x, axis=-1, keepdims=True) + NORM_EPS)
    r1 = x * rho1
    n1 = (r1 * gain_one).astype(BF16)
    qkv = jnp.dot(n1, wqkv, preferred_element_type=F32).astype(BF16)
    heads = qkv.reshape(seqs, LEN, 3, HEADS, HEAD_DIM)
    q, k, v = heads[:, :, 0], heads[:, :, 1], heads[:, :, 2]
    s = jnp.einsum("sihc,sjhc->shij", q, k, preferred_element_type=F32) * scale + full_bias
    shifted = jnp.exp(s - jnp.max(s, axis=-1, keepdims=True))
    p = shifted / jnp.sum(shifted, axis=-1, keepdims=True)
    p_b = p.astype(BF16)
    attn = jnp.einsum("shij,sjhc->sihc", p_b, v, preferred_element_type=F32)
    attn = attn.reshape(seqs * LEN, WIDTH).astype(BF16)
    h1 = x + jnp.dot(attn, wattn, preferred_element_type=F32)
    rho2 = lax.rsqrt(jnp.mean(h1 * h1, axis=-1, keepdims=True) + NORM_EPS)
    r2 = h1 * rho2
    n2 = (r2 * gain_two).astype(BF16)
    n2f = n2.astype(F32)
    logits = jnp.dot(n2f, router, precision=HIGH)
    probs = jax.nn.softmax(logits, axis=-1)
    onehot = (
        expert_ids[:, None] == lax.broadcasted_iota(jnp.int32, (seqs * LEN, EXPERTS), 1)
    ).astype(F32)
    gate = jnp.sum(probs * onehot, axis=-1, keepdims=True)
    deo = (gate * cotangent).astype(BF16)

    target = expert_ids * CAP + slots
    columns = lax.broadcasted_iota(jnp.int32, (seqs * LEN, EXPERTS * CAP), 1)
    route = ((target[:, None] == columns) & (slots[:, None] < CAP)).astype(BF16)
    route = route.reshape(seqs, LEN, EXPERTS * CAP)
    both = jnp.stack([n2.reshape(seqs, LEN, WIDTH), deo.reshape(seqs, LEN, WIDTH)])
    sent = jnp.einsum("stc,kstd->kscd", route, both, preferred_element_type=F32).astype(BF16)
    sent = sent.reshape(2, seqs, EXPERTS, CAP, WIDTH).transpose(2, 0, 1, 3, 4)
    arrived = exchange(sent.reshape(EXPERTS, 2 * seqs * CAP, WIDTH), 2, "to_experts")
    arrived = arrived.reshape(EXPERTS, 2, seqs * CAP, WIDTH)
    rows = arrived[:, 0].reshape(EXPERTS * seqs * CAP, WIDTH)
    drows = arrived[:, 1].reshape(EXPERTS * seqs * CAP, WIDTH)

    pre = contract_last(rows, all_in)
    activated, gelu_back = jax.vjp(jax.nn.gelu, pre)
    hid = activated.astype(BF16)
    eo = jnp.dot(hid, all_out, preferred_element_type=F32).astype(BF16)
    dhid = contract_last(drows, all_out)
    dpre = gelu_back(dhid)[0].astype(BF16)
    dn2e = jnp.dot(dpre, all_in, preferred_element_type=F32).astype(BF16)
    gin = contract_first(dpre, rows).astype(BF16)
    gout = contract_first(hid, drows).astype(BF16)

    back = jnp.stack(
        [
            eo.reshape(EXPERTS, seqs * CAP, WIDTH),
            dn2e.reshape(EXPERTS, seqs * CAP, WIDTH),
        ],
        axis=1,
    )
    back = exchange(back.reshape(EXPERTS, 2 * seqs * CAP, WIDTH), 3, "from_experts")
    back = back.reshape(EXPERTS, 2, seqs, CAP, WIDTH).transpose(1, 2, 0, 3, 4)
    back = back.reshape(2, seqs, EXPERTS * CAP, WIDTH)
    combined = jnp.einsum("stc,kscd->kstd", route, back, preferred_element_type=F32)
    combined = combined.reshape(2, seqs * LEN, WIDTH)
    output = h1 + gate * combined[0]
    dgate = jnp.sum(cotangent * combined[0], axis=-1, keepdims=True)
    dlogits = probs * (onehot - gate) * dgate
    grad_router = lax.dot_general(n2f, dlogits, (((0,), (0,)), ((), ())), precision=HIGH)
    dn2 = lax.dot_general(dlogits, router, (((1,), (1,)), ((), ())), precision=HIGH) + combined[1]
    grad_gain_two = jnp.sum(dn2 * r2, axis=0)
    u2 = dn2 * gain_two
    dh1 = cotangent + rho2 * (u2 - r2 * jnp.mean(u2 * r2, axis=-1, keepdims=True))
    da = dh1.astype(BF16)
    grad_attn = contract_first(attn, da)
    dattn = contract_last(da, wattn).astype(BF16).reshape(seqs, LEN, HEADS, HEAD_DIM)
    dv = jnp.einsum("shij,sihc->sjhc", p_b, dattn, preferred_element_type=F32)
    dp = jnp.einsum("sihc,sjhc->shij", dattn, v, preferred_element_type=F32)
    ds = p * (dp - jnp.sum(p * dp, axis=-1, keepdims=True))
    grad_bias = jnp.einsum("bij,hij->bh", bucket_onehot, jnp.sum(ds, axis=0), precision=HIGH)
    ds_b = ds.astype(BF16)
    dq = jnp.einsum("shij,sjhc->sihc", ds_b, k, preferred_element_type=F32) * scale
    dk = jnp.einsum("shij,sihc->sjhc", ds_b, q, preferred_element_type=F32) * scale
    dqkv = jnp.stack([dq, dk, dv], axis=2).reshape(seqs * LEN, 3 * WIDTH).astype(BF16)
    grad_qkv = contract_first(n1, dqkv)
    dn1 = contract_last(dqkv, wqkv)
    grad_gain_one = jnp.sum(dn1 * r1, axis=0)
    u1 = dn1 * gain_one
    grad_tokens = dh1 + rho1 * (u1 - r1 * jnp.mean(u1 * r1, axis=-1, keepdims=True))

    dgrads = jnp.concatenate([grad_qkv, grad_attn], axis=1).astype(BF16)
    dgrads = dgrads.reshape(WIDTH, EXPERTS, COLS).transpose(1, 0, 2)
    small = jnp.concatenate(
        [
            grad_router.reshape(128, 48),
            grad_gain_one.reshape(128, 6),
            grad_gain_two.reshape(128, 6),
            grad_bias.reshape(128, 3),
            jnp.zeros((128, 65), F32),
        ],
        axis=1,
    ).reshape(DP, 8, 128)
    small = jnp.concatenate([small, jnp.zeros((DP, 8, 128), F32)], axis=1)
    grad_in, grad_out, dense_out, small = reduce(
        gin.reshape(DP, SHARD, WIDTH), gout.reshape(DP, SHARD, WIDTH), dgrads, small
    )
    dense_out = dense_out[:, :18].reshape(EXPERTS, 3, 6, 128).transpose(2, 0, 1, 3)
    dense_out = dense_out.reshape(6, EXPERTS * COLS)
    small = lax.dynamic_index_in_dim(small, me, 0, keepdims=False)
    return (
        output,
        grad_tokens,
        dense_out[:, : 3 * WIDTH],
        dense_out[:, 3 * WIDTH :],
        small[:48].reshape(6, EXPERTS),
        small[48:54],
        small[54:60],
        small[60:63],
        grad_in[None],
        grad_out[None],
    )


def solution(mesh):
    spread = ("dp", "expert")
    in_specs = (
        P(spread, None),
        P(spread, None),
        P(spread, None),
        P(spread, None),
        P(spread),
        P(spread),
        P(spread),
        P("expert", "dp", None),
        P("expert", "dp", None),
        P(spread),
        P(spread),
        P(),
        P(spread, None),
    )
    out_specs = (
        P(spread, None),
        P(spread, None),
        P(spread, None),
        P(spread, None),
        P(spread, None),
        P(spread),
        P(spread),
        P(spread),
        P("expert", "dp", None),
        P("expert", "dp", None),
    )
    return jax.shard_map(local, mesh=mesh, in_specs=in_specs, out_specs=out_specs, check_vma=False)
```

```python
import math

import jax
import jax.numpy as jnp
import numpy as np
from jax import lax
from jax.experimental import pallas as pl
from jax.experimental.pallas import tpu as pltpu
from jax.sharding import PartitionSpec as P

MESH = pl.DeviceIdType.MESH
HEADS = 12
HEAD_DIM = 64
BUCKETS = 32
LEN = 128
WIDTH = 768
FF = 3072
EXPERTS = 8
DP = 16
CAP = 16
SHARD = FF // DP
COLS = 384
ROWS = 48
NORM_EPS = 1e-06
HIGH = lax.Precision.HIGHEST
F32 = jnp.float32
BF16 = jnp.bfloat16
MIB = 1 << 20


def place_matrix():
    m = np.zeros((160, 384), np.float32)
    for c in range(3):
        for e in range(8):
            for r in range(6):
                m[c * 48 + e * 6 + r, e * 48 + c * 6 + r] = 1
    for e in range(8):
        m[144 + e, e * 48 + 32] = 1
    return m


def spread_matrix():
    m = np.zeros((256, 144), np.float32)
    for c in range(3):
        for e in range(8):
            for r in range(6):
                m[e * 32 + c * 6 + r, c * 48 + e * 6 + r] = 1
    return m


def small_matrices():
    n = np.arange(WIDTH)
    owner = np.zeros((128, WIDTH), np.float32)
    owner[n // 6, n] = 1
    gains = np.zeros((2, 128, WIDTH), np.float32)
    gains[0, 48 + n % 6, n] = 1
    gains[1, 56 + n % 6, n] = 1
    col = np.arange(128)
    group = ((col[None] // 8 == n[:, None] % 6) & (col[None] < 48)).astype(np.float32)
    fold = np.zeros((128, 128), np.float32)
    fold[np.arange(48), np.arange(48) % 8] = 1
    table = np.zeros((128, 128), np.float32)
    for j in range(4):
        for b in range(BUCKETS):
            table[4 * b + j, j * 32 + b] = 1
    pick = np.zeros((4, 16, 128), np.float32)
    for j in range(4):
        for t in range(3):
            pick[j, 3 * j + t, 64 + t] = 1
    return owner, gains, group, fold, table, pick


class Where:
    def __init__(self):
        self.dp = lax.axis_index("dp")
        self.e = lax.axis_index("expert")
        self.z, self.y = lax.div(self.dp, 4), lax.rem(self.dp, 4)
        self.x, self.c = lax.div(self.e, 2), lax.rem(self.e, 2)
        self.partner_e = self.x * 2 + (1 - self.c)
        self.partner = {"expert": self.partner_e}

    def at(self, axis, step):
        if axis == "y":
            return self.z * 4 + lax.rem(self.y + step + 4, 4)
        if axis == "z":
            return lax.rem(self.z + step + 4, 4) * 4 + self.y
        return lax.rem(self.x + step + 4, 4) * 2 + self.c

    def dev(self, axis, step):
        return {"expert" if axis == "x" else "dp": self.at(axis, step)}

    def at2(self, axis1, step1, step2):
        dy, dz = (step1, step2) if axis1 == "y" else (step2, step1)
        return lax.rem(self.z + dz + 4, 4) * 4 + lax.rem(self.y + dy + 4, 4)


def greet(w, dp_too):
    barrier = pltpu.get_barrier_semaphore()

    def hello_e(k, n):
        pl.semaphore_signal(
            barrier, inc=1, device_id={"expert": lax.rem(w.e + k, EXPERTS)}, device_id_type=MESH
        )
        return n

    def hello_dp(k, n):
        pl.semaphore_signal(
            barrier, inc=1, device_id={"dp": lax.rem(w.dp + k, DP)}, device_id_type=MESH
        )
        return n

    lax.fori_loop(1, EXPERTS, hello_e, 0)
    if dp_too:
        lax.fori_loop(1, DP, hello_dp, 0)
    pl.semaphore_wait(barrier, EXPERTS - 1 + (DP - 1 if dp_too else 0))


def remote(src, dst, send, recv, dev):
    return pltpu.make_async_remote_copy(
        src_ref=src, dst_ref=dst, send_sem=send, recv_sem=recv, device_id=dev, device_id_type=MESH
    )


class RingGather:
    def __init__(self, w, axis, place, rows, send, recv, base, own=None):
        self.w, self.axis, self.place, self.half = w, axis, place, rows // 2
        self.send, self.recv, self.base = send, recv, base
        self.own = place(0) if own is None else own
        self.copies = []

    def _go(self, k, src, dst, step):
        copy = remote(
            src,
            dst,
            self.send.at[self.base + k],
            self.recv.at[self.base + k],
            self.w.dev(self.axis, step),
        )
        copy.start()
        self.copies.append(copy)

    def start(self):
        self._go(0, self.own, self.place(0), 1)
        self._go(1, self.own, self.place(0), -1)

    def relay(self):
        h = self.half
        self.copies[0].wait_recv()
        low = self.place(-1).at[pl.ds(0, h)]
        self._go(2, low, low, 1)
        self.copies[1].wait_recv()
        high = self.place(1).at[pl.ds(h, h)]
        self._go(3, high, high, -1)

    def finish(self):
        self.copies[2].wait_recv()
        self.copies[3].wait_recv()

    def drain(self):
        for copy in self.copies:
            copy.wait_send()


def add_rows(rows, step, dst, *srcs):
    def body(i, n):
        part = pl.ds(pl.multiple_of(i * step, step), step)
        total = srcs[0][part].astype(F32)
        for src in srcs[1:]:
            total = total + src[part].astype(F32)
        dst[part] = total.astype(dst.dtype)
        return n

    lax.fori_loop(0, rows // step, body, 0)


class RingSum:
    def __init__(self, w, axis, place, rows, relayed, landed, send, recv, base):
        self.w, self.axis, self.place, self.rows, self.half = w, axis, place, rows, rows // 2
        self.relayed, self.landed = relayed, landed
        self.send, self.recv, self.base = send, recv, base
        self.copies = {}

    def _go(self, k, src, dst, step):
        copy = remote(
            src,
            dst,
            self.send.at[self.base + k],
            self.recv.at[self.base + k],
            self.w.dev(self.axis, step),
        )
        copy.start()
        self.copies[k] = copy

    def _part(self, ref, k):
        return ref.at[pl.ds(k * self.half, self.half)]

    def far(self):
        self._go(0, self._part(self.place(2), 0), self.relayed.at[0], 1)
        self._go(1, self._part(self.place(2), 1), self.relayed.at[1], -1)

    def near(self):
        self._go(2, self._part(self.place(1), 1), self._part(self.landed.at[0], 1), 1)
        self._go(3, self._part(self.place(-1), 0), self._part(self.landed.at[1], 0), -1)

    def relay(self):
        self.copies[0].wait_recv()
        low = self._part(self.place(1), 0)
        add_rows(self.half, 32, low, low, self.relayed.at[0])
        self._go(4, low, self._part(self.landed.at[0], 0), 1)
        self.copies[1].wait_recv()
        high = self._part(self.place(-1), 1)
        add_rows(self.half, 32, high, high, self.relayed.at[1])
        self._go(5, high, self._part(self.landed.at[1], 1), -1)

    def finish(self, dst):
        for k in (2, 3, 4, 5):
            self.copies[k].wait_recv()
        add_rows(self.rows, 32, dst, self.place(0), self.landed.at[0], self.landed.at[1])

    def drain(self):
        for k in range(6):
            self.copies[k].wait_send()


def contract_last(left, right):
    return lax.dot_general(left, right, (((1,), (1,)), ((), ())), preferred_element_type=F32)


def contract_first(left, right):
    return lax.dot_general(left, right, (((0,), (0,)), ((), ())), preferred_element_type=F32)


def gelu_both(v):
    c = math.sqrt(2.0 / math.pi)
    square = v * v
    t = jnp.tanh(c * v * (1.0 + 0.044715 * square))
    half = 0.5 * (1.0 + t)
    slope = half + 0.5 * v * (1.0 - t * t) * (c * (1.0 + (3.0 * 0.044715) * square))
    return v * half, slope


def exact_dot(left, right):
    return jnp.dot(left, right, precision=HIGH, preferred_element_type=F32)


def layer_kernel(
    x_ref,
    cot_ref,
    ids_ref,
    slots_ref,
    buckets_ref,
    first_ref,
    place_ref,
    spread_ref,
    owner_ref,
    gains_ref,
    group_ref,
    fold_ref,
    table_ref,
    pick_ref,
    win_ref,
    wout_ref,
    output_ref,
    grad_tokens_ref,
    in_ref,
    out_ref,
    dense_out_ref,
    extra_out_ref,
    weights,
    dense,
    extra,
    got,
    piece,
    extra_piece,
    qkv,
    attn,
    n1,
    n2,
    h1,
    probs,
    gate,
    p_all,
    bias,
    router,
    gain,
    sent,
    arrived,
    back,
    returned,
    eo,
    dn2e,
    grads,
    relayed,
    landed,
    ddense,
    crossed,
    x_relayed,
    x_landed,
    dp_got,
    dp_extra,
    extra_mine,
    extra_sum,
    last,
    last_got,
    extra_got,
    da,
    dattn,
    dqkv,
    ds_sum,
    dlogits,
    gain_grads,
    bias_rows,
    own_sem,
    a2a_send,
    a2a_recv,
    dp_send,
    dp_recv,
    ring_send,
    ring_recv,
    x_send,
    x_recv,
    tok_send,
    tok_recv,
    sum_send,
    sum_recv,
    sx_send,
    sx_recv,
    sdp_send,
    sdp_recv,
    sa_send,
    sa_recv,
):
    w = Where()
    scale = HEAD_DIM ** (-0.5)
    greet(w, True)

    def to_expert(k):
        peer = lax.rem(w.e + k, EXPERTS)
        return remote(
            first_ref.at[peer], got.at[w.e], a2a_send.at[k], a2a_recv.at[k], {"expert": peer}
        )

    def start_a2a(k, n):
        to_expert(k).start()
        return n

    lax.fori_loop(1, EXPERTS, start_a2a, 0)
    got[w.e] = first_ref[w.e]
    owns = []
    one, two = {}, {}
    for n, (own, axis1, axis2) in enumerate(((win_ref, "y", "z"), (wout_ref, "z", "y"))):
        keep = pltpu.make_async_copy(own, weights.at[n, w.dp], own_sem.at[n])
        keep.start()
        owns.append(keep)
        one[n] = RingGather(
            w,
            axis1,
            lambda s, n=n, a=axis1: weights.at[n, w.at2(a, s, 0)],
            SHARD,
            ring_send,
            ring_recv,
            n * 20,
            own=own,
        )
        for k, o in enumerate((0, -1, 1, 2)):
            two[n, o] = RingGather(
                w,
                axis2,
                lambda s, n=n, a=axis1, o=o: weights.at[n, w.at2(a, o, s)],
                SHARD,
                ring_send,
                ring_recv,
                n * 20 + 4 + 4 * k,
                own=own if o == 0 else None,
            )
    for n in range(2):
        one[n].start()

    def end_a2a(k, n):
        copy = to_expert(k)
        copy.wait_recv()
        copy.wait_send()
        return n

    lax.fori_loop(1, EXPERTS, end_a2a, 0)
    placed = jnp.dot(place_ref[...], got[...].reshape(384, 128), preferred_element_type=F32).astype(
        BF16
    )
    for c in range(3):
        piece[:, c * 128 : (c + 1) * 128] = placed[c * 48 : (c + 1) * 48]
    extra_piece[...] = placed[144:160]
    mine = pl.ds(pl.multiple_of(w.dp * ROWS, 16), ROWS)

    def to_dp(k):
        dev = {"dp": lax.rem(w.dp + k, DP)}
        return (
            remote(piece, dense.at[w.e, mine], dp_send.at[0, k], dp_recv.at[0, k], dev),
            remote(extra_piece, extra.at[w.dp], dp_send.at[1, k], dp_recv.at[1, k], dev),
        )

    def start_dp(k, n):
        for copy in to_dp(k):
            copy.start()
        return n

    def end_dp(k, n):
        for copy in to_dp(k):
            copy.wait_recv()
            copy.wait_send()
        return n

    lax.fori_loop(1, DP, start_dp, 0)
    dense[w.e, mine] = piece[...]
    extra[w.dp] = extra_piece[...]
    for n in range(2):
        two[n, 0].start()
    x = x_ref[...].astype(F32)
    rho1 = lax.rsqrt(jnp.mean(x * x, axis=-1, keepdims=True) + NORM_EPS)
    lax.fori_loop(1, DP, end_dp, 0)
    ring = RingGather(w, "x", lambda s: dense.at[w.at("x", s)], WIDTH, x_send, x_recv, 0)
    ring.start()

    def across(k, ref):
        copy = remote(ref, ref, x_send.at[4 + k], x_recv.at[4 + k], w.partner)
        copy.start()
        return copy

    pair = [across(0, dense.at[w.e])]
    for n in range(2):
        one[n].relay()
        two[n, -1].start()
        two[n, 1].start()

    small = extra[...].astype(F32)[:, :8].reshape(128, 128).astype(BF16)
    owner = owner_ref[...]
    for n in range(2):
        tiled = jnp.dot(small, gains_ref[n], preferred_element_type=F32)
        gain[n : n + 1] = jnp.sum(tiled * owner.astype(F32), axis=0, keepdims=True)
    rows_small = contract_first(owner, small) * group_ref[...].astype(F32)
    router[...] = jnp.dot(
        rows_small.astype(BF16), fold_ref[...], preferred_element_type=F32
    ).astype(BF16)
    tables = contract_first(small, table_ref[...])
    buckets = buckets_ref[...]
    for h in range(HEADS):
        row = tables[64 + h % 3 : 65 + h % 3]
        bias[h] = jnp.take_along_axis(
            jnp.broadcast_to(row, (LEN, 128)), buckets + 32 * (h // 3), axis=1
        )
    n1[...] = (x * rho1 * gain[0:1]).astype(BF16)

    ring.relay()
    pair.append(across(1, dense.at[w.at("x", -1)]))
    pair.append(across(2, dense.at[w.at("x", 1)]))
    for n in range(2):
        two[n, 0].relay()
    for n in range(2):
        one[n].finish()
        two[n, 2].start()
    ring.finish()
    pair.append(across(3, dense.at[w.at("x", 2)]))
    for copy in pair:
        copy.wait_recv()
    for e in range(6):
        qkv[:, e * COLS : (e + 1) * COLS] = jnp.dot(
            n1[...], dense[e], preferred_element_type=F32
        ).astype(BF16)

    low_lanes = lax.broadcasted_iota(jnp.int32, (LEN, 128), 1) < HEAD_DIM
    lanes_of = (low_lanes, jnp.logical_not(low_lanes))
    zero = jnp.zeros((LEN, 128), BF16)

    def lanes_at(block, hp):
        return pl.ds(pl.multiple_of(block * WIDTH + hp * 128, 128), 128)

    def attention(s, lo, hi):
        rows = pl.ds(s * LEN, LEN)

        def pairs(i, n):
            for u in range(2):
                hp = 2 * i + u
                q, k, v = (qkv[rows, lanes_at(b, hp)] for b in range(3))
                outs = []
                for t in range(2):
                    h = 2 * hp + t
                    logit = contract_last(jnp.where(lanes_of[t], q, zero), k) * scale + bias[h]
                    shifted = jnp.exp(logit - jnp.max(logit, axis=-1, keepdims=True))
                    p = shifted / jnp.sum(shifted, axis=-1, keepdims=True)
                    p_all[s * HEADS + h] = p
                    outs.append(jnp.dot(p.astype(BF16), v, preferred_element_type=F32))
                attn[rows, lanes_at(0, hp)] = jnp.where(low_lanes, outs[0], outs[1]).astype(BF16)
            return n

        lax.fori_loop(lo, hi, pairs, 0)

    expert_lane = lax.broadcasted_iota(jnp.int32, (LEN, 128), 1)
    expert_row = lax.broadcasted_iota(jnp.int32, (LEN, 128), 0)
    eye16 = (
        lax.broadcasted_iota(jnp.int32, (16, 128), 0) == lax.broadcasted_iota(jnp.int32, (16, 128), 1)
    ).astype(BF16)

    def routing(s):
        ids, slots = ids_ref[s : s + 1], slots_ref[s : s + 1]
        target = jnp.where(slots < CAP, ids * CAP + slots, -1)
        route = (jnp.broadcast_to(target, (LEN, 128)) == expert_row).astype(F32).astype(BF16)
        hot_t = (
            (jnp.broadcast_to(ids, (16, LEN)) == lax.broadcasted_iota(jnp.int32, (16, LEN), 0))
            .astype(F32)
            .astype(BF16)
        )
        return route, contract_first(hot_t, eye16)

    def second_norm(s):
        rows = pl.ds(s * LEN, LEN)
        for e in range(2):
            cols = pl.ds(e * COLS, COLS)
            h1[rows, cols] = x_ref[rows, cols].astype(F32) + jnp.dot(
                attn[rows], dense[6 + e], preferred_element_type=F32
            )
        h = h1[rows]
        rho2 = lax.rsqrt(jnp.mean(h * h, axis=-1, keepdims=True) + NORM_EPS)
        normed = (h * rho2 * gain[1:2]).astype(BF16)
        n2[rows] = normed
        logits = jnp.dot(normed, router[...], preferred_element_type=F32)
        logits = jnp.where(expert_lane < EXPERTS, logits, -1e30)
        raised = jnp.exp(logits - jnp.max(logits, axis=-1, keepdims=True))
        prob = raised / jnp.sum(raised, axis=-1, keepdims=True)
        route, hot = routing(s)
        g = jnp.sum(prob * hot, axis=-1, keepdims=True)
        probs[rows] = prob
        gate[rows] = jnp.broadcast_to(g, (LEN, 128))
        deo = (g * cot_ref[rows]).astype(BF16)
        for kind, value in enumerate((normed, deo)):
            picked = jnp.dot(route, value, preferred_element_type=F32).astype(BF16)
            for e in range(EXPERTS):
                sent[s, e, kind] = picked[e * CAP : (e + 1) * CAP]

    def token_copy(src, dst, base, s, k):
        peer = lax.rem(w.e + k, EXPERTS)
        at = base + s * EXPERTS + k
        return remote(
            src.at[s, peer], dst.at[s, w.e], tok_send.at[at], tok_recv.at[at], {"expert": peer}
        )

    def send_tokens(src, dst, base, s):
        def begin(k, n):
            token_copy(src, dst, base, s, k).start()
            return n

        lax.fori_loop(1, EXPERTS, begin, 0)
        dst[s, w.e] = src[s, w.e]

    def wait_tokens(src, dst, base, s):
        def end(k, n):
            copy = token_copy(src, dst, base, s, k)
            copy.wait_recv()
            copy.wait_send()
            return n

        lax.fori_loop(1, EXPERTS, end, 0)

    attention(0, 0, 3)
    second_norm(0)
    send_tokens(sent, arrived, 0, 0)
    for n in range(2):
        two[n, -1].relay()
        two[n, 1].relay()
    attention(1, 0, 3)
    second_norm(1)
    send_tokens(sent, arrived, 0, 1)
    for n in range(2):
        two[n, 2].relay()
    for n in range(2):
        for o in (0, -1, 1, 2):
            two[n, o].finish()
    for s in range(2):
        wait_tokens(sent, arrived, 0, s)
    for copy in owns:
        copy.wait()

    slots_here = 2 * EXPERTS * CAP
    eo[...] = jnp.zeros_like(eo)
    dn2e[...] = jnp.zeros_like(dn2e)

    def hidden_block(j, n):
        block = pl.ds(2 * j, 2)
        w_in = weights[0, block].reshape(2 * SHARD, WIDTH)
        w_out = weights[1, block].reshape(2 * SHARD, WIDTH)
        rows = arrived[:, :, 0].reshape(slots_here, WIDTH)
        drows = arrived[:, :, 1].reshape(slots_here, WIDTH)
        act, slope = gelu_both(contract_last(rows, w_in))
        hid = act.astype(BF16)
        dpre = (contract_last(drows, w_out) * slope).astype(BF16)
        eo[...] += jnp.dot(hid, w_out, preferred_element_type=F32)
        dn2e[...] += jnp.dot(dpre, w_in, preferred_element_type=F32)
        grads[0, block] = contract_first(dpre, rows).astype(BF16).reshape(2, SHARD, WIDTH)
        grads[1, block] = contract_first(hid, drows).astype(BF16).reshape(2, SHARD, WIDTH)
        return n

    lax.fori_loop(0, DP // 2, hidden_block, 0)
    for s in range(2):
        for e in range(EXPERTS):
            rows = pl.ds((s * EXPERTS + e) * CAP, CAP)
            back[s, e, 0] = eo[rows].astype(BF16)
            back[s, e, 1] = dn2e[rows].astype(BF16)
        send_tokens(back, returned, 16, s)

    axes = (("y", "z"), ("z", "y"))
    order = (2, 1, -1, 0)
    sum1, sum2 = {}, {}
    for n, (axis1, axis2) in enumerate(axes):
        for k, o in enumerate(order):
            sum2[n, o] = RingSum(
                w,
                axis2,
                lambda s, n=n, a=axis1, o=o: grads.at[n, w.at2(a, o, s)],
                SHARD,
                relayed.at[n * 5 + k],
                landed.at[n * 5 + k],
                sum_send,
                sum_recv,
                (n * 5 + k) * 6,
            )
        sum1[n] = RingSum(
            w,
            axis1,
            lambda s, n=n, a=axis1: grads.at[n, w.at2(a, s, 0)],
            SHARD,
            relayed.at[n * 5 + 4],
            landed.at[n * 5 + 4],
            sum_send,
            sum_recv,
            (n * 5 + 4) * 6,
        )
    for o in order:
        for n in range(2):
            sum2[n, o].far()
    for o in order:
        for n in range(2):
            sum2[n, o].near()
    for n in range(2):
        sum2[n, 2].relay()

    gain_grads[...] = jnp.zeros_like(gain_grads)

    def second_norm_back(s):
        rows = pl.ds(s * LEN, LEN)
        route, hot = routing(s)
        combined = contract_first(route, returned[s, :, 0].reshape(LEN, WIDTH))
        g, cot, h = gate[rows, 0:1], cot_ref[rows], h1[rows]
        output_ref[rows] = h + g * combined
        dgate = jnp.sum(cot * combined, axis=-1, keepdims=True)
        dl = (probs[rows] * (hot - g) * dgate).astype(BF16)
        dlogits[rows] = dl
        dn2 = contract_last(dl, router[...]) + contract_first(
            route, returned[s, :, 1].reshape(LEN, WIDTH)
        )
        rho2 = lax.rsqrt(jnp.mean(h * h, axis=-1, keepdims=True) + NORM_EPS)
        r2 = h * rho2
        gain_grads[1:2] += jnp.sum(dn2 * r2, axis=0, keepdims=True)
        u2 = dn2 * gain[1:2]
        dh1 = cot + rho2 * (u2 - r2 * jnp.mean(u2 * r2, axis=-1, keepdims=True))
        h1[rows] = dh1
        da[rows] = dh1.astype(BF16)
        total = contract_last(da[rows, 0:COLS], dense[6])
        dattn[rows] = (total + contract_last(da[rows, COLS:WIDTH], dense[7])).astype(BF16)

    def attention_back(s, lo, hi):
        rows = pl.ds(s * LEN, LEN)

        def pairs(i, n):
            for u in range(2):
                hp = 2 * i + u
                q, k, v = (qkv[rows, lanes_at(b, hp)] for b in range(3))
                d_out = dattn[rows, lanes_at(0, hp)]
                dqs, dks, dvs = [], [], []
                for t in range(2):
                    h = 2 * hp + t
                    p = p_all[s * HEADS + h]
                    dprob = contract_last(jnp.where(lanes_of[t], d_out, zero), v)
                    ds = p * (dprob - jnp.sum(p * dprob, axis=-1, keepdims=True))
                    if s == 1:
                        ds_sum[h] = ds
                    else:
                        ds_sum[h] += ds
                    ds_b = ds.astype(BF16)
                    dvs.append(contract_first(p.astype(BF16), d_out))
                    dqs.append(jnp.dot(ds_b, k, preferred_element_type=F32))
                    dks.append(contract_first(ds_b, q))
                dqkv[rows, lanes_at(0, hp)] = (
                    jnp.where(low_lanes, dqs[0], dqs[1]) * scale
                ).astype(BF16)
                dqkv[rows, lanes_at(1, hp)] = (
                    jnp.where(low_lanes, dks[0], dks[1]) * scale
                ).astype(BF16)
                dqkv[rows, lanes_at(2, hp)] = jnp.where(low_lanes, dvs[0], dvs[1]).astype(BF16)
            return n

        lax.fori_loop(lo, hi, pairs, 0)

    wait_tokens(back, returned, 16, 1)
    second_norm_back(1)
    attention_back(1, 0, 3)
    for o in (1, -1):
        for n in range(2):
            sum2[n, o].relay()
    wait_tokens(back, returned, 16, 0)
    second_norm_back(0)
    for e in range(2):
        ddense[6 + e] = contract_first(attn[...], da[:, e * COLS : (e + 1) * COLS]).astype(BF16)
    for n in range(2):
        sum2[n, 0].relay()
    attention_back(0, 0, 3)
    for n in range(2):
        sum2[n, 2].finish(grads.at[n, w.at2(axes[n][0], 2, 0)])
        sum1[n].far()
    for e in range(6):
        ddense[e] = contract_first(n1[...], dqkv[:, e * COLS : (e + 1) * COLS]).astype(BF16)

    pair_sum = []
    for k in range(4):
        copy = remote(
            ddense.at[2 * k + 1 - w.c],
            crossed.at[k],
            sx_send.at[6 + k],
            sx_recv.at[6 + k],
            w.partner,
        )
        copy.start()
        pair_sum.append(copy)
    for n in range(2):
        for o in (1, -1):
            sum2[n, o].finish(grads.at[n, w.at2(axes[n][0], o, 0)])
        sum1[n].near()
    for k in range(4):
        pair_sum[k].wait_recv()
        add_rows(WIDTH, 32, ddense.at[2 * k + w.c], ddense.at[2 * k + w.c], crossed.at[k])
    xsum = RingSum(
        w, "x", lambda s: ddense.at[w.at("x", s)], WIDTH, x_relayed, x_landed, sx_send, sx_recv, 0
    )
    xsum.far()
    xsum.near()

    dn1 = contract_last(dqkv[:, 0:COLS], dense[0])
    for e in range(1, 6):
        dn1 = dn1 + contract_last(dqkv[:, e * COLS : (e + 1) * COLS], dense[e])
    x = x_ref[...].astype(F32)
    rho1 = lax.rsqrt(jnp.mean(x * x, axis=-1, keepdims=True) + NORM_EPS)
    r1 = x * rho1
    gain_grads[0:1] = jnp.sum(dn1 * r1, axis=0, keepdims=True)
    u1 = dn1 * gain[0:1]
    grad_tokens_ref[...] = h1[...] + rho1 * (
        u1 - r1 * jnp.mean(u1 * r1, axis=-1, keepdims=True)
    )
    for n in range(2):
        sum1[n].relay()
    xsum.relay()

    def bucket(b, n):
        hit = (buckets_ref[...] == b)[None]
        bias_rows[b] = jnp.sum(jnp.where(hit, ds_sum[...], 0.0), axis=1)
        return n

    lax.fori_loop(0, BUCKETS, bucket, 0)
    per_bucket = jnp.sum(bias_rows[...], axis=2)
    per_bucket = jnp.concatenate([per_bucket, jnp.zeros((BUCKETS, 4), F32)], axis=1)
    owner_f = owner_ref[...].astype(F32)
    grad_router = contract_first(n2[...], dlogits[...])
    wide = lax.dot_general(
        grad_router,
        fold_ref[...].astype(F32),
        (((1,), (1,)), ((), ())),
        precision=HIGH,
        preferred_element_type=F32,
    ) * group_ref[...].astype(F32)
    smalls = exact_dot(owner_f, wide)
    for n in range(2):
        smalls = smalls + lax.dot_general(
            owner_f * gain_grads[n : n + 1],
            gains_ref[n].astype(F32),
            (((1,), (1,)), ((), ())),
            precision=HIGH,
            preferred_element_type=F32,
        )
    table = table_ref[...].astype(F32)
    for j in range(4):
        smalls = smalls + exact_dot(
            table[:, j * 32 : (j + 1) * 32], exact_dot(per_bucket, pick_ref[j].astype(F32))
        )
    extra_mine[...] = smalls.reshape(DP, 8, 128)

    def extra_dp(k):
        peer = lax.rem(w.dp + k, DP)
        return remote(
            extra_mine.at[peer],
            dp_extra.at[w.dp],
            sdp_send.at[1, k],
            sdp_recv.at[1, k],
            {"dp": peer},
        )

    def start_extra(k, n):
        extra_dp(k).start()
        return n

    lax.fori_loop(1, DP, start_extra, 0)
    dp_extra[w.dp] = extra_mine[w.dp]
    for n in range(2):
        sum2[n, 0].finish(grads.at[n, w.dp])
    xsum.finish(ddense.at[w.e])

    def rows_of(dp):
        return pl.ds(pl.multiple_of(dp * ROWS, 16), ROWS)

    def dense_dp(k):
        peer = lax.rem(w.dp + k, DP)
        return remote(
            ddense.at[w.e, rows_of(peer)],
            dp_got.at[w.dp],
            sdp_send.at[0, k],
            sdp_recv.at[0, k],
            {"dp": peer},
        )

    def start_dense(k, n):
        dense_dp(k).start()
        return n

    def end_dense(k, n):
        for copy in (dense_dp(k), extra_dp(k)):
            copy.wait_recv()
            copy.wait_send()
        return n

    lax.fori_loop(1, DP, start_dense, 0)
    dp_got[w.dp] = ddense[w.e, rows_of(w.dp)]
    for n, ref in ((0, in_ref), (1, out_ref)):
        sum1[n].finish(ref)
    lax.fori_loop(1, DP, end_dense, 0)
    total = dp_got[0].astype(F32)
    extra_total = dp_extra[0]
    for k in range(1, DP):
        total = total + dp_got[k].astype(F32)
        extra_total = extra_total + dp_extra[k]
    extra_sum[...] = extra_total
    flat = jnp.concatenate([total[:, c * 128 : (c + 1) * 128] for c in range(3)], axis=0)
    last[...] = (
        jnp.dot(spread_ref[...], flat.astype(BF16), preferred_element_type=F32)
        .astype(BF16)
        .reshape(EXPERTS, 32, 128)
    )

    def to_owner(k):
        peer = lax.rem(w.e + k, EXPERTS)
        dev = {"expert": peer}
        return (
            remote(last.at[peer], last_got.at[w.e], sa_send.at[0, k], sa_recv.at[0, k], dev),
            remote(extra_sum, extra_got.at[w.e], sa_send.at[1, k], sa_recv.at[1, k], dev),
        )

    def start_owner(k, n):
        for copy in to_owner(k):
            copy.start()
        return n

    def end_owner(k, n):
        for copy in to_owner(k):
            copy.wait_recv()
            copy.wait_send()
        return n

    lax.fori_loop(1, EXPERTS, start_owner, 0)
    last_got[w.e] = last[w.e]
    extra_got[w.e] = extra_sum[...]
    lax.fori_loop(1, EXPERTS, end_owner, 0)
    dense_out_ref[...] = last_got[...].astype(F32)
    extra_total = extra_got[0]
    for k in range(1, EXPERTS):
        extra_total = extra_total + extra_got[k]
    extra_out_ref[...] = extra_total

    for copy in pair:
        copy.wait_send()
    ring.drain()
    for n in range(2):
        one[n].drain()
        for o in (0, -1, 1, 2):
            two[n, o].drain()
    for copy in pair_sum:
        copy.wait_send()
    xsum.drain()
    for n in range(2):
        sum1[n].drain()
        for o in order:
            sum2[n, o].drain()


def layer(x, cot, ids, slots, buckets, first, win, wout):
    hbm = pl.BlockSpec(memory_space=pl.ANY)
    vmem = pl.BlockSpec(memory_space=pltpu.VMEM)
    tokens = x.shape[0]
    half = SHARD // 2
    small = tuple(jnp.asarray(m, BF16) for m in (place_matrix(), spread_matrix(), *small_matrices()))

    def dma(*shape):
        return pltpu.SemaphoreType.DMA(shape)

    return pl.pallas_call(
        layer_kernel,
        out_shape=(
            jax.ShapeDtypeStruct((tokens, WIDTH), F32),
            jax.ShapeDtypeStruct((tokens, WIDTH), F32),
            jax.ShapeDtypeStruct((SHARD, WIDTH), F32),
            jax.ShapeDtypeStruct((SHARD, WIDTH), F32),
            jax.ShapeDtypeStruct((EXPERTS, 32, 128), F32),
            jax.ShapeDtypeStruct((8, 128), F32),
        ),
        in_specs=[vmem] * 14 + [hbm, hbm],
        out_specs=(vmem,) * 6,
        scratch_shapes=[
            pltpu.VMEM((2, DP, SHARD, WIDTH), BF16),
            pltpu.VMEM((EXPERTS, WIDTH, COLS), BF16),
            pltpu.VMEM((DP, 16, 128), BF16),
            pltpu.VMEM((EXPERTS, 48, 128), BF16),
            pltpu.VMEM((ROWS, COLS), BF16),
            pltpu.VMEM((16, 128), BF16),
            pltpu.VMEM((tokens, 3 * WIDTH), BF16),
            pltpu.VMEM((tokens, WIDTH), BF16),
            pltpu.VMEM((tokens, WIDTH), BF16),
            pltpu.VMEM((tokens, WIDTH), BF16),
            pltpu.VMEM((tokens, WIDTH), F32),
            pltpu.VMEM((tokens, 128), F32),
            pltpu.VMEM((tokens, 128), F32),
            pltpu.VMEM((2 * HEADS, LEN, LEN), F32),
            pltpu.VMEM((HEADS, LEN, LEN), F32),
            pltpu.VMEM((WIDTH, 128), BF16),
            pltpu.VMEM((8, WIDTH), F32),
            pltpu.VMEM((2, EXPERTS, 2, CAP, WIDTH), BF16),
            pltpu.VMEM((2, EXPERTS, 2, CAP, WIDTH), BF16),
            pltpu.VMEM((2, EXPERTS, 2, CAP, WIDTH), BF16),
            pltpu.VMEM((2, EXPERTS, 2, CAP, WIDTH), BF16),
            pltpu.VMEM((tokens, WIDTH), F32),
            pltpu.VMEM((tokens, WIDTH), F32),
            pltpu.VMEM((2, DP, SHARD, WIDTH), BF16),
            pltpu.VMEM((10, 2, half, WIDTH), BF16),
            pltpu.VMEM((10, 2, SHARD, WIDTH), BF16),
            pltpu.VMEM((EXPERTS, WIDTH, COLS), BF16),
            pltpu.VMEM((4, WIDTH, COLS), BF16),
            pltpu.VMEM((2, WIDTH // 2, COLS), BF16),
            pltpu.VMEM((2, WIDTH, COLS), BF16),
            pltpu.VMEM((DP, ROWS, COLS), BF16),
            pltpu.VMEM((DP, 8, 128), F32),
            pltpu.VMEM((DP, 8, 128), F32),
            pltpu.VMEM((8, 128), F32),
            pltpu.VMEM((EXPERTS, 32, 128), BF16),
            pltpu.VMEM((EXPERTS, 32, 128), BF16),
            pltpu.VMEM((EXPERTS, 8, 128), F32),
            pltpu.VMEM((tokens, WIDTH), BF16),
            pltpu.VMEM((tokens, WIDTH), BF16),
            pltpu.VMEM((tokens, 3 * WIDTH), BF16),
            pltpu.VMEM((HEADS, LEN, LEN), F32),
            pltpu.VMEM((tokens, 128), BF16),
            pltpu.VMEM((8, WIDTH), F32),
            pltpu.VMEM((BUCKETS, HEADS, LEN), F32),
            dma(2),
            dma(EXPERTS),
            dma(EXPERTS),
            dma(2, DP),
            dma(2, DP),
            dma(40),
            dma(40),
            dma(8),
            dma(8),
            dma(32),
            dma(32),
            dma(60),
            dma(60),
            dma(10),
            dma(10),
            dma(2, DP),
            dma(2, DP),
            dma(2, EXPERTS),
            dma(2, EXPERTS),
        ],
        compiler_params=pltpu.CompilerParams(
            collective_id=0, has_side_effects=True, vmem_limit_bytes=63 * MIB
        ),
        name="layer",
    )(x, cot, ids, slots, buckets, first, *small, win, wout)


def local(
    tokens,
    w_qkv,
    w_attn_out,
    w_router,
    gain_attn,
    gain_moe,
    bias_table,
    w_in,
    w_out,
    expert_ids,
    slots,
    buckets,
    cotangent,
):
    seqs = tokens.shape[0] // LEN
    me = lax.axis_index("expert")
    dense = jnp.concatenate([w_qkv, w_attn_out], axis=1)
    first = dense.reshape(6, EXPERTS, 3, 128).transpose(1, 2, 0, 3).reshape(EXPERTS, 18, 128)
    gap = jnp.zeros((2,), BF16)
    small = jnp.concatenate(
        [w_router.reshape(48), gain_attn, gap, gain_moe, gap, bias_table, jnp.zeros((61,), BF16)]
    )
    small = jnp.broadcast_to(small[None, None], (EXPERTS, 1, 128))
    first = jnp.concatenate(
        [first, jnp.zeros((EXPERTS, 14, 128), BF16), small, jnp.zeros((EXPERTS, 15, 128), BF16)],
        axis=1,
    )
    output, grad_tokens, grad_in, grad_out, dense_out, small = layer(
        tokens,
        cotangent,
        expert_ids.reshape(seqs, LEN),
        slots.reshape(seqs, LEN),
        buckets,
        first,
        w_in[0],
        w_out[0],
    )
    dense_out = dense_out[:, :18].reshape(EXPERTS, 3, 6, 128).transpose(2, 0, 1, 3)
    dense_out = dense_out.reshape(6, EXPERTS * COLS)
    small = lax.dynamic_index_in_dim(small, me, 0, keepdims=False)
    return (
        output,
        grad_tokens,
        dense_out[:, : 3 * WIDTH],
        dense_out[:, 3 * WIDTH :],
        small[:48].reshape(6, EXPERTS),
        small[48:54],
        small[56:62],
        small[64:67],
        grad_in[None],
        grad_out[None],
    )


def solution(mesh):
    spread = ("dp", "expert")
    in_specs = (
        P(spread, None),
        P(spread, None),
        P(spread, None),
        P(spread, None),
        P(spread),
        P(spread),
        P(spread),
        P("expert", "dp", None),
        P("expert", "dp", None),
        P(spread),
        P(spread),
        P(),
        P(spread, None),
    )
    out_specs = (
        P(spread, None),
        P(spread, None),
        P(spread, None),
        P(spread, None),
        P(spread, None),
        P(spread),
        P(spread),
        P(spread),
        P("expert", "dp", None),
        P("expert", "dp", None),
    )
    return jax.shard_map(local, mesh=mesh, in_specs=in_specs, out_specs=out_specs, check_vma=False)
```

```python
import math

import jax
import jax.numpy as jnp
import numpy as np
from jax import lax
from jax.experimental import pallas as pl
from jax.experimental.pallas import tpu as pltpu
from jax.sharding import PartitionSpec as P

MESH = pl.DeviceIdType.MESH
HEADS = 12
HEAD_DIM = 64
BUCKETS = 32
LEN = 128
WIDTH = 768
FF = 3072
EXPERTS = 8
DP = 16
CAP = 16
SHARD = FF // DP
COLS = 384
ROWS = 48
NORM_EPS = 1e-06
HIGH = lax.Precision.HIGHEST
F32 = jnp.float32
BF16 = jnp.bfloat16
MIB = 1 << 20


def place_matrix():
    m = np.zeros((160, 384), np.float32)
    for c in range(3):
        for e in range(8):
            for r in range(6):
                m[c * 48 + e * 6 + r, e * 48 + c * 6 + r] = 1
    for e in range(8):
        m[144 + e, e * 48 + 32] = 1
    return m


def spread_matrix():
    m = np.zeros((256, 144), np.float32)
    for c in range(3):
        for e in range(8):
            for r in range(6):
                m[e * 32 + c * 6 + r, c * 48 + e * 6 + r] = 1
    return m


def small_matrices():
    n = np.arange(WIDTH)
    owner = np.zeros((128, WIDTH), np.float32)
    owner[n // 6, n] = 1
    gains = np.zeros((2, 128, WIDTH), np.float32)
    gains[0, 48 + n % 6, n] = 1
    gains[1, 56 + n % 6, n] = 1
    col = np.arange(128)
    group = ((col[None] // 8 == n[:, None] % 6) & (col[None] < 48)).astype(np.float32)
    fold = np.zeros((128, 128), np.float32)
    fold[np.arange(48), np.arange(48) % 8] = 1
    table = np.zeros((128, 128), np.float32)
    for j in range(4):
        for b in range(BUCKETS):
            table[4 * b + j, j * 32 + b] = 1
    pick = np.zeros((4, 16, 128), np.float32)
    for j in range(4):
        for t in range(3):
            pick[j, 3 * j + t, 64 + t] = 1
    return owner, gains, group, fold, table, pick


class Where:
    def __init__(self):
        self.dp = lax.axis_index("dp")
        self.e = lax.axis_index("expert")
        self.z, self.y = lax.div(self.dp, 4), lax.rem(self.dp, 4)
        self.x, self.c = lax.div(self.e, 2), lax.rem(self.e, 2)
        self.partner_e = self.x * 2 + (1 - self.c)
        self.partner = {"expert": self.partner_e}

    def at(self, axis, step):
        if axis == "y":
            return self.z * 4 + lax.rem(self.y + step + 4, 4)
        if axis == "z":
            return lax.rem(self.z + step + 4, 4) * 4 + self.y
        return lax.rem(self.x + step + 4, 4) * 2 + self.c

    def dev(self, axis, step):
        return {"expert" if axis == "x" else "dp": self.at(axis, step)}

    def at2(self, axis1, step1, step2):
        dy, dz = (step1, step2) if axis1 == "y" else (step2, step1)
        return lax.rem(self.z + dz + 4, 4) * 4 + lax.rem(self.y + dy + 4, 4)


def greet(w):
    barrier = pltpu.get_barrier_semaphore()

    def hello_e(k, n):
        pl.semaphore_signal(
            barrier, inc=1, device_id={"expert": lax.rem(w.e + k, EXPERTS)}, device_id_type=MESH
        )
        return n

    def hello_dp(k, n):
        pl.semaphore_signal(
            barrier, inc=1, device_id={"dp": lax.rem(w.dp + k, DP)}, device_id_type=MESH
        )
        return n

    lax.fori_loop(1, EXPERTS, hello_e, 0)
    lax.fori_loop(1, DP, hello_dp, 0)


def remote(src, dst, send, recv, dev):
    return pltpu.make_async_remote_copy(
        src_ref=src, dst_ref=dst, send_sem=send, recv_sem=recv, device_id=dev, device_id_type=MESH
    )


class FineRingGather:
    def __init__(self, w, axis, place, rows, send, recv):
        self.w, self.axis, self.place, self.half = w, axis, place, rows // 2
        self.send, self.recv = send, recv
        self.copies = []

    def _go(self, step, place, k):
        part = place.at[pl.ds(k * self.half, self.half)]
        n = len(self.copies)
        copy = remote(
            part, part, self.send.at[n], self.recv.at[n], self.w.dev(self.axis, step)
        )
        copy.start()
        self.copies.append(copy)

    def start(self):
        own = self.place(0)
        self._go(1, own, 0)
        self._go(-1, own, 1)
        self._go(1, own, 1)
        self._go(-1, own, 0)

    def relay(self):
        self.copies[0].wait_recv()
        self._go(1, self.place(-1), 0)
        self.copies[1].wait_recv()
        self._go(-1, self.place(1), 1)

    def near(self):
        self.copies[2].wait_recv()
        self.copies[3].wait_recv()

    def finish(self):
        self.copies[4].wait_recv()
        self.copies[5].wait_recv()

    def drain(self):
        for copy in self.copies:
            copy.wait_send()


class RingGather:
    def __init__(self, w, axis, place, rows, send, recv, base, own=None):
        self.w, self.axis, self.place, self.half = w, axis, place, rows // 2
        self.send, self.recv, self.base = send, recv, base
        self.own = place(0) if own is None else own
        self.copies = []

    def _go(self, k, src, dst, step):
        copy = remote(
            src,
            dst,
            self.send.at[self.base + k],
            self.recv.at[self.base + k],
            self.w.dev(self.axis, step),
        )
        copy.start()
        self.copies.append(copy)

    def start(self):
        self._go(0, self.own, self.place(0), 1)
        self._go(1, self.own, self.place(0), -1)

    def relay(self):
        h = self.half
        self.copies[0].wait_recv()
        low = self.place(-1).at[pl.ds(0, h)]
        self._go(2, low, low, 1)
        self.copies[1].wait_recv()
        high = self.place(1).at[pl.ds(h, h)]
        self._go(3, high, high, -1)

    def finish(self):
        self.copies[2].wait_recv()
        self.copies[3].wait_recv()

    def drain(self):
        for copy in self.copies:
            copy.wait_send()


def add_rows(rows, step, dst, *srcs):
    def body(i, n):
        part = pl.ds(pl.multiple_of(i * step, step), step)
        total = srcs[0][part].astype(F32)
        for src in srcs[1:]:
            total = total + src[part].astype(F32)
        dst[part] = total.astype(dst.dtype)
        return n

    lax.fori_loop(0, rows // step, body, 0)


class RingSum:
    def __init__(self, w, axis, place, rows, relayed, landed, send, recv, base):
        self.w, self.axis, self.place, self.rows, self.half = w, axis, place, rows, rows // 2
        self.relayed, self.landed = relayed, landed
        self.send, self.recv, self.base = send, recv, base
        self.step = min(32, self.half)
        self.copies = {}

    def _go(self, k, src, dst, step):
        copy = remote(
            src,
            dst,
            self.send.at[self.base + k],
            self.recv.at[self.base + k],
            self.w.dev(self.axis, step),
        )
        copy.start()
        self.copies[k] = copy

    def _part(self, ref, k):
        return ref.at[pl.ds(k * self.half, self.half)]

    def far(self):
        self._go(0, self._part(self.place(2), 0), self.relayed.at[0], 1)
        self._go(1, self._part(self.place(2), 1), self.relayed.at[1], -1)

    def near(self):
        self._go(2, self._part(self.place(1), 1), self._part(self.landed.at[0], 1), 1)
        self._go(3, self._part(self.place(-1), 0), self._part(self.landed.at[1], 0), -1)

    def relay(self):
        self.copies[0].wait_recv()
        low = self._part(self.place(1), 0)
        add_rows(self.half, self.step, low, low, self.relayed.at[0])
        self._go(4, low, self._part(self.landed.at[0], 0), 1)
        self.copies[1].wait_recv()
        high = self._part(self.place(-1), 1)
        add_rows(self.half, self.step, high, high, self.relayed.at[1])
        self._go(5, high, self._part(self.landed.at[1], 1), -1)

    def finish(self, dst):
        for k in (2, 3, 4, 5):
            self.copies[k].wait_recv()
        add_rows(self.rows, self.step, dst, self.place(0), self.landed.at[0], self.landed.at[1])

    def drain(self):
        for k in range(6):
            self.copies[k].wait_send()


def contract_last(left, right):
    return lax.dot_general(left, right, (((1,), (1,)), ((), ())), preferred_element_type=F32)


def contract_first(left, right):
    return lax.dot_general(left, right, (((0,), (0,)), ((), ())), preferred_element_type=F32)


def gelu_both(v):
    c = math.sqrt(2.0 / math.pi)
    square = v * v
    t = jnp.tanh(c * v * (1.0 + 0.044715 * square))
    half = 0.5 * (1.0 + t)
    slope = half + 0.5 * v * (1.0 - t * t) * (c * (1.0 + (3.0 * 0.044715) * square))
    return v * half, slope


def exact_dot(left, right):
    return jnp.dot(left, right, precision=HIGH, preferred_element_type=F32)


def layer_kernel(
    x_hbm,
    cot_hbm,
    ids_hbm,
    slots_hbm,
    buckets_hbm,
    wqkv_ref,
    wattn_ref,
    wrouter_ref,
    small_ref,
    place_hbm,
    spread_hbm,
    owner_hbm,
    gains_hbm,
    group_hbm,
    fold_hbm,
    table_hbm,
    pick_hbm,
    win_ref,
    wout_ref,
    output_hbm,
    grad_tokens_hbm,
    in_hbm,
    out_hbm,
    grad_qkv_ref,
    grad_attn_ref,
    router_out_ref,
    extra_out_ref,
    x_ref,
    cot_ref,
    ids_ref,
    slots_ref,
    buckets_ref,
    first_f,
    first_ref,
    place_ref,
    spread_ref,
    owner_ref,
    gains_ref,
    group_ref,
    fold_ref,
    table_ref,
    pick_ref,
    output_ref,
    grad_tokens_ref,
    in_ref,
    out_ref,
    weights,
    dense,
    extra,
    got,
    piece,
    extra_piece,
    qkv,
    attn,
    n1,
    n2,
    h1,
    probs,
    gate,
    p_all,
    bias,
    router,
    gain,
    sent,
    arrived,
    back,
    returned,
    eo,
    dn2e,
    grads,
    relayed,
    landed,
    ddense,
    dthird,
    crossed,
    crossed_third,
    x_relayed,
    x_landed,
    dp_got,
    third_relayed,
    third_landed,
    third_relayed_y,
    third_landed_y,
    third_sum,
    third_last,
    dp_extra,
    extra_mine,
    extra_sum,
    last,
    last_got,
    extra_got,
    da,
    dattn,
    dqkv,
    ds_sum,
    dlogits,
    gain_grads,
    bias_rows,
    load_sem,
    store_sem,
    own_sem,
    a2a_send,
    a2a_recv,
    dp_send,
    dp_recv,
    ring_send,
    ring_recv,
    x_send,
    x_recv,
    tok_send,
    tok_recv,
    sum_send,
    sum_recv,
    sx_send,
    sx_recv,
    sdp_send,
    sdp_recv,
    sa_send,
    sa_recv,
    st_send,
    st_recv,
):
    w = Where()
    scale = HEAD_DIM ** (-0.5)
    loads = [
        pltpu.make_async_copy(src, dst, load_sem.at[k])
        for k, (src, dst) in enumerate(
            (
                (fold_hbm, fold_ref),
                (place_hbm, place_ref),
                (x_hbm, x_ref),
                (owner_hbm, owner_ref),
                (gains_hbm, gains_ref),
                (group_hbm, group_ref),
                (table_hbm, table_ref),
                (buckets_hbm, buckets_ref),
                (ids_hbm, ids_ref),
                (slots_hbm, slots_ref),
                (cot_hbm, cot_ref),
                (pick_hbm, pick_ref),
                (spread_hbm, spread_ref),
            )
        )
    ]
    for load in loads:
        load.start()
    stores = []

    def store(src, dst):
        copy = pltpu.make_async_copy(src, dst, store_sem.at[len(stores)])
        copy.start()
        stores.append(copy)

    greet(w)
    loads[0].wait()

    first_f[...] = jnp.zeros_like(first_f)
    lane = lax.broadcasted_iota(jnp.int32, (6, 128), 1)
    turn = 8 * lax.broadcasted_iota(jnp.int32, (6, 128), 0)
    routed = contract_last(wrouter_ref[...], fold_ref[:, :EXPERTS])
    routed = jnp.where((lane >= turn) & (lane < turn + 8), routed, 0.0)
    row = jnp.sum(routed, axis=0, keepdims=True) + small_ref[...].astype(F32)
    for e in range(EXPERTS):
        ref, at = (wqkv_ref, e * COLS) if e < 6 else (wattn_ref, (e - 6) * COLS)
        for c in range(3):
            first_f[e, c * 6 : c * 6 + 6] = ref[:, at + c * 128 : at + (c + 1) * 128].astype(F32)
        first_f[e, 32:33] = row
    first_ref[...] = first_f[...].astype(BF16)
    pl.semaphore_wait(pltpu.get_barrier_semaphore(), EXPERTS - 1 + DP - 1)

    def to_expert(k):
        peer = lax.rem(w.e + k, EXPERTS)
        return remote(
            first_ref.at[peer], got.at[w.e], a2a_send.at[k], a2a_recv.at[k], {"expert": peer}
        )

    def start_a2a(k, n):
        to_expert(k).start()
        return n

    lax.fori_loop(1, EXPERTS, start_a2a, 0)
    got[w.e] = first_ref[w.e]
    owns = []
    one, two = {}, {}
    for n, (own, axis1, axis2) in enumerate(((win_ref, "y", "z"), (wout_ref, "z", "y"))):
        keep = pltpu.make_async_copy(own, weights.at[n, w.dp], own_sem.at[n])
        keep.start()
        owns.append(keep)
        one[n] = RingGather(
            w,
            axis1,
            lambda s, n=n, a=axis1: weights.at[n, w.at2(a, s, 0)],
            SHARD,
            ring_send,
            ring_recv,
            n * 20,
            own=own,
        )
        for k, o in enumerate((0, -1, 1, 2)):
            two[n, o] = RingGather(
                w,
                axis2,
                lambda s, n=n, a=axis1, o=o: weights.at[n, w.at2(a, o, s)],
                SHARD,
                ring_send,
                ring_recv,
                n * 20 + 4 + 4 * k,
                own=own if o == 0 else None,
            )
    for n in range(2):
        one[n].start()
    for load in loads[1:]:
        load.wait()

    def end_a2a(k, n):
        copy = to_expert(k)
        copy.wait_recv()
        copy.wait_send()
        return n

    lax.fori_loop(1, EXPERTS, end_a2a, 0)
    placed = jnp.dot(place_ref[...], got[...].reshape(384, 128), preferred_element_type=F32).astype(
        BF16
    )
    for c in range(3):
        piece[:, c * 128 : (c + 1) * 128] = placed[c * 48 : (c + 1) * 48]
    extra_piece[...] = placed[144:160]
    mine = pl.ds(pl.multiple_of(w.dp * ROWS, 16), ROWS)

    def to_dp(k):
        dev = {"dp": lax.rem(w.dp + k, DP)}
        return (
            remote(piece, dense.at[w.e, mine], dp_send.at[0, k], dp_recv.at[0, k], dev),
            remote(extra_piece, extra.at[w.dp], dp_send.at[1, k], dp_recv.at[1, k], dev),
        )

    def start_dp(k, n):
        for copy in to_dp(k):
            copy.start()
        return n

    def end_dp(k, n):
        for copy in to_dp(k):
            copy.wait_recv()
            copy.wait_send()
        return n

    lax.fori_loop(1, DP, start_dp, 0)
    dense[w.e, mine] = piece[...]
    extra[w.dp] = extra_piece[...]
    for n in range(2):
        two[n, 0].start()
    x = x_ref[...].astype(F32)
    rho1 = lax.rsqrt(jnp.mean(x * x, axis=-1, keepdims=True) + NORM_EPS)
    lax.fori_loop(1, DP, end_dp, 0)
    ring = FineRingGather(w, "x", lambda s: dense.at[w.at("x", s)], WIDTH, x_send, x_recv)
    ring.start()

    def across(k, ref):
        copy = remote(ref, ref, x_send.at[6 + k], x_recv.at[6 + k], w.partner)
        copy.start()
        return copy

    pair = [across(0, dense.at[w.e])]
    for n in range(2):
        one[n].relay()
        two[n, -1].start()
        two[n, 1].start()

    small = extra[...].astype(F32)[:, :8].reshape(128, 128).astype(BF16)
    owner = owner_ref[...]
    for n in range(2):
        tiled = jnp.dot(small, gains_ref[n], preferred_element_type=F32)
        gain[n : n + 1] = jnp.sum(tiled * owner.astype(F32), axis=0, keepdims=True)
    rows_small = contract_first(owner, small) * group_ref[...].astype(F32)
    router[...] = jnp.dot(
        rows_small.astype(BF16), fold_ref[...], preferred_element_type=F32
    ).astype(BF16)
    tables = contract_first(small, table_ref[...])
    buckets = buckets_ref[...]
    for h in range(HEADS):
        row = tables[64 + h % 3 : 65 + h % 3]
        bias[h] = jnp.take_along_axis(
            jnp.broadcast_to(row, (LEN, 128)), buckets + 32 * (h // 3), axis=1
        )
    n1[...] = (x * rho1 * gain[0:1]).astype(BF16)

    ring.relay()
    ring.near()
    pair.append(across(1, dense.at[w.at("x", -1)]))
    pair.append(across(2, dense.at[w.at("x", 1)]))
    for n in range(2):
        two[n, 0].relay()
    for n in range(2):
        one[n].finish()
        two[n, 2].start()
    ring.finish()
    pair.append(across(3, dense.at[w.at("x", 2)]))
    for copy in pair:
        copy.wait_recv()
    for e in range(6):
        qkv[:, e * COLS : (e + 1) * COLS] = jnp.dot(
            n1[...], dense[e], preferred_element_type=F32
        ).astype(BF16)

    low_lanes = lax.broadcasted_iota(jnp.int32, (LEN, 128), 1) < HEAD_DIM
    lanes_of = (low_lanes, jnp.logical_not(low_lanes))
    zero = jnp.zeros((LEN, 128), BF16)

    def lanes_at(block, hp):
        return pl.ds(pl.multiple_of(block * WIDTH + hp * 128, 128), 128)

    def attention(s, lo, hi):
        rows = pl.ds(s * LEN, LEN)

        def pairs(i, n):
            for u in range(2):
                hp = 2 * i + u
                q, k, v = (qkv[rows, lanes_at(b, hp)] for b in range(3))
                outs = []
                for t in range(2):
                    h = 2 * hp + t
                    logit = contract_last(jnp.where(lanes_of[t], q, zero), k) * scale + bias[h]
                    shifted = jnp.exp(logit - jnp.max(logit, axis=-1, keepdims=True))
                    p = shifted / jnp.sum(shifted, axis=-1, keepdims=True)
                    p_all[s * HEADS + h] = p
                    outs.append(jnp.dot(p.astype(BF16), v, preferred_element_type=F32))
                attn[rows, lanes_at(0, hp)] = jnp.where(low_lanes, outs[0], outs[1]).astype(BF16)
            return n

        lax.fori_loop(lo, hi, pairs, 0)

    expert_lane = lax.broadcasted_iota(jnp.int32, (LEN, 128), 1)
    expert_row = lax.broadcasted_iota(jnp.int32, (LEN, 128), 0)
    eye16 = (
        lax.broadcasted_iota(jnp.int32, (16, 128), 0) == lax.broadcasted_iota(jnp.int32, (16, 128), 1)
    ).astype(BF16)

    def routing(s):
        ids, slots = ids_ref[s : s + 1], slots_ref[s : s + 1]
        target = jnp.where(slots < CAP, ids * CAP + slots, -1)
        route = (jnp.broadcast_to(target, (LEN, 128)) == expert_row).astype(F32).astype(BF16)
        hot_t = (
            (jnp.broadcast_to(ids, (16, LEN)) == lax.broadcasted_iota(jnp.int32, (16, LEN), 0))
            .astype(F32)
            .astype(BF16)
        )
        return route, contract_first(hot_t, eye16)

    def second_norm(s):
        rows = pl.ds(s * LEN, LEN)
        for e in range(2):
            cols = pl.ds(e * COLS, COLS)
            h1[rows, cols] = x_ref[rows, cols].astype(F32) + jnp.dot(
                attn[rows], dense[6 + e], preferred_element_type=F32
            )
        h = h1[rows]
        rho2 = lax.rsqrt(jnp.mean(h * h, axis=-1, keepdims=True) + NORM_EPS)
        normed = (h * rho2 * gain[1:2]).astype(BF16)
        n2[rows] = normed
        logits = jnp.dot(normed, router[...], preferred_element_type=F32)
        logits = jnp.where(expert_lane < EXPERTS, logits, -1e30)
        raised = jnp.exp(logits - jnp.max(logits, axis=-1, keepdims=True))
        prob = raised / jnp.sum(raised, axis=-1, keepdims=True)
        route, hot = routing(s)
        g = jnp.sum(prob * hot, axis=-1, keepdims=True)
        probs[rows] = prob
        gate[rows] = jnp.broadcast_to(g, (LEN, 128))
        deo = (g * cot_ref[rows]).astype(BF16)
        for kind, value in enumerate((normed, deo)):
            picked = jnp.dot(route, value, preferred_element_type=F32).astype(BF16)
            for e in range(EXPERTS):
                sent[s, e, kind] = picked[e * CAP : (e + 1) * CAP]

    def token_copy(src, dst, base, s, k):
        peer = lax.rem(w.e + k, EXPERTS)
        at = base + s * EXPERTS + k
        return remote(
            src.at[s, peer], dst.at[s, w.e], tok_send.at[at], tok_recv.at[at], {"expert": peer}
        )

    def send_tokens(src, dst, base, s):
        def begin(k, n):
            token_copy(src, dst, base, s, k).start()
            return n

        lax.fori_loop(1, EXPERTS, begin, 0)
        dst[s, w.e] = src[s, w.e]

    def wait_tokens(src, dst, base, s):
        def end(k, n):
            copy = token_copy(src, dst, base, s, k)
            copy.wait_recv()
            copy.wait_send()
            return n

        lax.fori_loop(1, EXPERTS, end, 0)

    attention(0, 0, 3)
    second_norm(0)
    send_tokens(sent, arrived, 0, 0)
    for n in range(2):
        two[n, -1].relay()
        two[n, 1].relay()
    attention(1, 0, 3)
    second_norm(1)
    send_tokens(sent, arrived, 0, 1)
    for n in range(2):
        two[n, 2].relay()
    for n in range(2):
        for o in (0, -1, 1, 2):
            two[n, o].finish()
    for s in range(2):
        wait_tokens(sent, arrived, 0, s)
    for copy in owns:
        copy.wait()

    axes = (("y", "z"), ("z", "y"))
    order = (2, 1, -1, 0)
    sum1, sum2 = {}, {}
    for n, (axis1, axis2) in enumerate(axes):
        for k, o in enumerate(order):
            sum2[n, o] = RingSum(
                w,
                axis2,
                lambda s, n=n, a=axis1, o=o: grads.at[n, w.at2(a, o, s)],
                SHARD,
                relayed.at[n * 5 + k],
                landed.at[n * 5 + k],
                sum_send,
                sum_recv,
                (n * 5 + k) * 6,
            )
        sum1[n] = RingSum(
            w,
            axis1,
            lambda s, n=n, a=axis1: grads.at[n, w.at2(a, s, 0)],
            SHARD,
            relayed.at[n * 5 + 4],
            landed.at[n * 5 + 4],
            sum_send,
            sum_recv,
            (n * 5 + 4) * 6,
        )
    slots_here = 2 * EXPERTS * CAP
    eo[...] = jnp.zeros_like(eo)
    dn2e[...] = jnp.zeros_like(dn2e)


    def hidden_blocks(one_of, other_of):
        def body(i, n):
            at = [w.at2("y", dy, dz) for dz, dy in (one_of(i), other_of(i))]
            w_in = jnp.concatenate([weights[0, k] for k in at], axis=0)
            w_out = jnp.concatenate([weights[1, k] for k in at], axis=0)
            rows = arrived[:, :, 0].reshape(slots_here, WIDTH)
            drows = arrived[:, :, 1].reshape(slots_here, WIDTH)
            act, slope = gelu_both(contract_last(rows, w_in))
            hid = act.astype(BF16)
            dpre = (contract_last(drows, w_out) * slope).astype(BF16)
            eo[...] += jnp.dot(hid, w_out, preferred_element_type=F32)
            dn2e[...] += jnp.dot(dpre, w_in, preferred_element_type=F32)
            for m, value in enumerate((contract_first(dpre, rows), contract_first(hid, drows))):
                value = value.astype(BF16)
                for k in range(2):
                    grads[m, at[k]] = value[k * SHARD : (k + 1) * SHARD]
            return n

        lax.fori_loop(0, 2, body, 0)

    hidden_blocks(lambda i: (2, 2 * i), lambda i: (2, 2 * i + 1))
    for o in order:
        sum2[0, o].far()
    hidden_blocks(lambda i: (3 * i, 2), lambda i: (1, 2 - 2 * i))
    for o in order:
        sum2[1, o].far()
    hidden_blocks(lambda i: (0, i), lambda i: (3, i))
    hidden_blocks(lambda i: (1, 1 + 2 * i), lambda i: (3 * i, 3))
    for s in (1, 0):
        for e in range(EXPERTS):
            rows = pl.ds((s * EXPERTS + e) * CAP, CAP)
            back[s, e, 0] = eo[rows].astype(BF16)
            back[s, e, 1] = dn2e[rows].astype(BF16)
        send_tokens(back, returned, 16, s)

    for o in order:
        for n in range(2):
            sum2[n, o].near()
    for n in range(2):
        sum2[n, 2].relay()

    gain_grads[...] = jnp.zeros_like(gain_grads)

    def second_norm_back(s):
        rows = pl.ds(s * LEN, LEN)
        route, hot = routing(s)
        combined = contract_first(route, returned[s, :, 0].reshape(LEN, WIDTH))
        g, cot, h = gate[rows, 0:1], cot_ref[rows], h1[rows]
        output_ref[rows] = h + g * combined
        store(output_ref.at[rows], output_hbm.at[rows])
        dgate = jnp.sum(cot * combined, axis=-1, keepdims=True)
        dl = (probs[rows] * (hot - g) * dgate).astype(BF16)
        dlogits[rows] = dl
        dn2 = contract_last(dl, router[...]) + contract_first(
            route, returned[s, :, 1].reshape(LEN, WIDTH)
        )
        rho2 = lax.rsqrt(jnp.mean(h * h, axis=-1, keepdims=True) + NORM_EPS)
        r2 = h * rho2
        gain_grads[1:2] += jnp.sum(dn2 * r2, axis=0, keepdims=True)
        u2 = dn2 * gain[1:2]
        dh1 = cot + rho2 * (u2 - r2 * jnp.mean(u2 * r2, axis=-1, keepdims=True))
        h1[rows] = dh1
        da[rows] = dh1.astype(BF16)
        total = contract_last(da[rows, 0:COLS], dense[6])
        dattn[rows] = (total + contract_last(da[rows, COLS:WIDTH], dense[7])).astype(BF16)

    def attention_back(s, lo, hi):
        rows = pl.ds(s * LEN, LEN)

        def pairs(i, n):
            for u in range(2):
                hp = 2 * i + u
                q, k, v = (qkv[rows, lanes_at(b, hp)] for b in range(3))
                d_out = dattn[rows, lanes_at(0, hp)]
                dqs, dks, dvs = [], [], []
                for t in range(2):
                    h = 2 * hp + t
                    p = p_all[s * HEADS + h]
                    dprob = contract_last(jnp.where(lanes_of[t], d_out, zero), v)
                    ds = p * (dprob - jnp.sum(p * dprob, axis=-1, keepdims=True))
                    if s == 1:
                        ds_sum[h] = ds
                    else:
                        ds_sum[h] += ds
                    ds_b = ds.astype(BF16)
                    dvs.append(contract_first(p.astype(BF16), d_out))
                    dqs.append(jnp.dot(ds_b, k, preferred_element_type=F32))
                    dks.append(contract_first(ds_b, q))
                dqkv[rows, lanes_at(0, hp)] = (
                    jnp.where(low_lanes, dqs[0], dqs[1]) * scale
                ).astype(BF16)
                dqkv[rows, lanes_at(1, hp)] = (
                    jnp.where(low_lanes, dks[0], dks[1]) * scale
                ).astype(BF16)
                dqkv[rows, lanes_at(2, hp)] = jnp.where(low_lanes, dvs[0], dvs[1]).astype(BF16)
            return n

        lax.fori_loop(lo, hi, pairs, 0)

    wait_tokens(back, returned, 16, 1)
    second_norm_back(1)
    for o in (1, -1, 0):
        for n in range(2):
            sum2[n, o].relay()
    attention_back(1, 0, 3)
    wait_tokens(back, returned, 16, 0)
    second_norm_back(0)
    attention_back(0, 0, 3)

    third = 2 * COLS // 3

    def dense_block(e, value):
        value = value.astype(BF16)
        ddense[e] = value[:, :third]
        dthird[e % 2, :, e // 2] = value[:, third:].reshape(DP, ROWS, COLS - third)

    for e in range(6):
        dense_block(e, contract_first(n1[...], dqkv[:, e * COLS : (e + 1) * COLS]))
    for e in range(2):
        dense_block(6 + e, contract_first(attn[...], da[:, e * COLS : (e + 1) * COLS]))

    pair_third = remote(
        dthird.at[1 - w.c], crossed_third, sx_send.at[10], sx_recv.at[10], w.partner
    )
    pair_third.start()
    pair_sum = []
    for k, o in enumerate(order):
        to = lax.rem(w.x + o + 4, 4)
        copy = remote(
            ddense.at[2 * to + 1 - w.c],
            crossed.at[to],
            sx_send.at[6 + k],
            sx_recv.at[6 + k],
            w.partner,
        )
        copy.start()
        pair_sum.append(copy)

    def third_rows(s):
        return dthird.at[w.c, pl.ds(4 * lax.rem(w.z + s + 4, 4), 4)]

    zsum = RingSum(w, "z", third_rows, 4, third_relayed, third_landed, st_send, st_recv, 3)
    ysum = RingSum(
        w,
        "y",
        lambda s: dthird.at[w.c, w.at("y", s)],
        4,
        third_relayed_y,
        third_landed_y,
        st_send,
        st_recv,
        9,
    )

    def add_third(k, n):
        total = dthird[w.c, k].astype(F32) + crossed_third[k].astype(F32)
        dthird[w.c, k] = total.astype(BF16)
        return n

    def add_pair(k):
        pair_sum[k].wait_recv()
        to = lax.rem(w.x + order[k] + 4, 4)
        here = ddense.at[2 * to + w.c]
        add_rows(WIDTH, 32, here, here, crossed.at[to])

    pair_third.wait_recv()
    lax.fori_loop(0, DP, add_third, 0)
    zsum.far()
    zsum.near()
    xsum = RingSum(
        w, "x", lambda s: ddense.at[w.at("x", s)], WIDTH, x_relayed, x_landed, sx_send, sx_recv, 0
    )
    add_pair(0)
    xsum.far()
    add_pair(1)
    add_pair(2)
    xsum.near()
    add_pair(3)

    dn1 = contract_last(dqkv[:, 0:COLS], dense[0])
    for e in range(1, 6):
        dn1 = dn1 + contract_last(dqkv[:, e * COLS : (e + 1) * COLS], dense[e])
    x = x_ref[...].astype(F32)
    rho1 = lax.rsqrt(jnp.mean(x * x, axis=-1, keepdims=True) + NORM_EPS)
    r1 = x * rho1
    gain_grads[0:1] = jnp.sum(dn1 * r1, axis=0, keepdims=True)
    u1 = dn1 * gain[0:1]
    grad_tokens_ref[...] = h1[...] + rho1 * (
        u1 - r1 * jnp.mean(u1 * r1, axis=-1, keepdims=True)
    )
    store(grad_tokens_ref, grad_tokens_hbm)
    zsum.relay()
    for n in range(2):
        sum2[n, 2].finish(grads.at[n, w.at2(axes[n][0], 2, 0)])
        sum1[n].far()

    def bucket(b, n):
        hit = (buckets_ref[...] == b)[None]
        bias_rows[b] = jnp.sum(jnp.where(hit, ds_sum[...], 0.0), axis=1)
        return n

    lax.fori_loop(0, BUCKETS, bucket, 0)
    per_bucket = jnp.sum(bias_rows[...], axis=2)
    per_bucket = jnp.concatenate([per_bucket, jnp.zeros((BUCKETS, 4), F32)], axis=1)
    owner_f = owner_ref[...].astype(F32)
    grad_router = contract_first(n2[...], dlogits[...])
    wide = lax.dot_general(
        grad_router,
        fold_ref[...].astype(F32),
        (((1,), (1,)), ((), ())),
        precision=HIGH,
        preferred_element_type=F32,
    ) * group_ref[...].astype(F32)
    smalls = exact_dot(owner_f, wide)
    for n in range(2):
        smalls = smalls + lax.dot_general(
            owner_f * gain_grads[n : n + 1],
            gains_ref[n].astype(F32),
            (((1,), (1,)), ((), ())),
            precision=HIGH,
            preferred_element_type=F32,
        )
    table = table_ref[...].astype(F32)
    for j in range(4):
        smalls = smalls + exact_dot(
            table[:, j * 32 : (j + 1) * 32], exact_dot(per_bucket, pick_ref[j].astype(F32))
        )
    extra_mine[...] = smalls.reshape(DP, 8, 128)

    def extra_dp(k):
        peer = lax.rem(w.dp + k, DP)
        return remote(
            extra_mine.at[peer],
            dp_extra.at[w.dp],
            sdp_send.at[1, k],
            sdp_recv.at[1, k],
            {"dp": peer},
        )

    def start_extra(k, n):
        extra_dp(k).start()
        return n

    lax.fori_loop(1, DP, start_extra, 0)
    dp_extra[w.dp] = extra_mine[w.dp]
    zsum.finish(third_rows(0))
    ysum.far()
    ysum.near()
    xsum.relay()
    for n in range(2):
        for o in (1, -1):
            sum2[n, o].finish(grads.at[n, w.at2(axes[n][0], o, 0)])
        sum1[n].near()
    for n in range(2):
        sum1[n].relay()
    for n in range(2):
        sum2[n, 0].finish(grads.at[n, w.dp])
    ysum.relay()
    ysum.finish(third_sum)
    third_x = []
    for k, o in enumerate((2, 1, -1)):
        copy = remote(
            third_sum.at[lax.rem(w.x + o + 4, 4)],
            third_last.at[w.x],
            st_send.at[k],
            st_recv.at[k],
            w.dev("x", o),
        )
        copy.start()
        third_x.append(copy)
    third_last[w.x] = third_sum[w.x]
    xsum.finish(ddense.at[w.e])

    def rows_of(dp):
        return pl.ds(pl.multiple_of(dp * ROWS, 16), ROWS)

    def dense_dp(k):
        peer = lax.rem(w.dp + k, DP)
        return remote(
            ddense.at[w.e, rows_of(peer)],
            dp_got.at[w.dp],
            sdp_send.at[0, k],
            sdp_recv.at[0, k],
            {"dp": peer},
        )

    def start_dense(k, n):
        dense_dp(k).start()
        return n

    def end_dense(k, n):
        for copy in (dense_dp(k), extra_dp(k)):
            copy.wait_recv()
            copy.wait_send()
        return n

    lax.fori_loop(1, DP, start_dense, 0)
    dp_got[w.dp] = ddense[w.e, rows_of(w.dp)]
    for n, (ref, hbm) in enumerate(((in_ref, in_hbm), (out_ref, out_hbm))):
        sum1[n].finish(ref)
        store(ref, hbm)
    for copy in third_x:
        copy.wait_recv()
    last_third = third_last[0].astype(F32)
    for k in range(1, 4):
        last_third = last_third + third_last[k].astype(F32)
    lax.fori_loop(1, DP, end_dense, 0)
    total = dp_got[0].astype(F32)
    extra_total = dp_extra[0]
    for k in range(1, DP):
        total = total + dp_got[k].astype(F32)
        extra_total = extra_total + dp_extra[k]
    extra_sum[...] = extra_total
    flat = jnp.concatenate([total[:, :128], total[:, 128:], last_third], axis=0)
    last[...] = (
        jnp.dot(spread_ref[...], flat.astype(BF16), preferred_element_type=F32)
        .astype(BF16)
        .reshape(EXPERTS, 32, 128)
    )

    def to_owner(k):
        peer = lax.rem(w.e + k, EXPERTS)
        dev = {"expert": peer}
        return (
            remote(last.at[peer], last_got.at[w.e], sa_send.at[0, k], sa_recv.at[0, k], dev),
            remote(extra_sum, extra_got.at[w.e], sa_send.at[1, k], sa_recv.at[1, k], dev),
        )

    def start_owner(k, n):
        for copy in to_owner(k):
            copy.start()
        return n

    def end_owner(k, n):
        for copy in to_owner(k):
            copy.wait_recv()
            copy.wait_send()
        return n

    lax.fori_loop(1, EXPERTS, start_owner, 0)
    last_got[w.e] = last[w.e]
    extra_got[w.e] = extra_sum[...]
    lax.fori_loop(1, EXPERTS, end_owner, 0)
    for e in range(EXPERTS):
        columns = last_got[e].astype(F32)
        for c in range(3):
            ref = grad_qkv_ref if e < 6 else grad_attn_ref
            at = (e % 6 if e < 6 else e - 6) * COLS + c * 128
            ref[:, at : at + 128] = columns[c * 6 : c * 6 + 6]
    extra_total = extra_got[0]
    for k in range(1, EXPERTS):
        extra_total = extra_total + extra_got[k]
    extra_sum[...] = extra_total
    row = extra_sum[pl.ds(w.e, 1)]
    extra_out_ref[...] = row
    for r in range(6):
        router_out_ref[r : r + 1] = row[:, r * EXPERTS : (r + 1) * EXPERTS]

    for copy in pair:
        copy.wait_send()
    ring.drain()
    for n in range(2):
        one[n].drain()
        for o in (0, -1, 1, 2):
            two[n, o].drain()
    for copy in (*pair_sum, pair_third, *third_x):
        copy.wait_send()
    xsum.drain()
    zsum.drain()
    ysum.drain()
    for copy in stores:
        copy.wait()
    for n in range(2):
        sum1[n].drain()
        for o in order:
            sum2[n, o].drain()


def layer(x, cot, ids, slots, buckets, wqkv, wattn, wrouter, row, win, wout):
    hbm = pl.BlockSpec(memory_space=pl.ANY)
    vmem = pl.BlockSpec(memory_space=pltpu.VMEM)
    tokens = x.shape[0]
    half, main = SHARD // 2, COLS - 128
    small = tuple(jnp.asarray(m, BF16) for m in (place_matrix(), spread_matrix(), *small_matrices()))

    def dma(*shape):
        return pltpu.SemaphoreType.DMA(shape)

    return pl.pallas_call(
        layer_kernel,
        out_shape=(
            jax.ShapeDtypeStruct((tokens, WIDTH), F32),
            jax.ShapeDtypeStruct((tokens, WIDTH), F32),
            jax.ShapeDtypeStruct((SHARD, WIDTH), F32),
            jax.ShapeDtypeStruct((SHARD, WIDTH), F32),
            jax.ShapeDtypeStruct((6, 3 * WIDTH), F32),
            jax.ShapeDtypeStruct((6, WIDTH), F32),
            jax.ShapeDtypeStruct((6, EXPERTS), F32),
            jax.ShapeDtypeStruct((1, 128), F32),
        ),
        in_specs=[hbm] * 5 + [vmem] * 4 + [hbm] * 10,
        out_specs=(hbm,) * 4 + (vmem,) * 4,
        scratch_shapes=[
            *(pltpu.VMEM(a.shape, a.dtype) for a in (x, cot, ids, slots, buckets)),
            pltpu.VMEM((EXPERTS, ROWS, 128), F32),
            pltpu.VMEM((EXPERTS, ROWS, 128), BF16),
            *(pltpu.VMEM(a.shape, a.dtype) for a in small),
            pltpu.VMEM((tokens, WIDTH), F32),
            pltpu.VMEM((tokens, WIDTH), F32),
            pltpu.VMEM((SHARD, WIDTH), F32),
            pltpu.VMEM((SHARD, WIDTH), F32),
            pltpu.VMEM((2, DP, SHARD, WIDTH), BF16),
            pltpu.VMEM((EXPERTS, WIDTH, COLS), BF16),
            pltpu.VMEM((DP, 16, 128), BF16),
            pltpu.VMEM((EXPERTS, 48, 128), BF16),
            pltpu.VMEM((ROWS, COLS), BF16),
            pltpu.VMEM((16, 128), BF16),
            pltpu.VMEM((tokens, 3 * WIDTH), BF16),
            pltpu.VMEM((tokens, WIDTH), BF16),
            pltpu.VMEM((tokens, WIDTH), BF16),
            pltpu.VMEM((tokens, WIDTH), BF16),
            pltpu.VMEM((tokens, WIDTH), F32),
            pltpu.VMEM((tokens, 128), F32),
            pltpu.VMEM((tokens, 128), F32),
            pltpu.VMEM((2 * HEADS, LEN, LEN), F32),
            pltpu.VMEM((HEADS, LEN, LEN), F32),
            pltpu.VMEM((WIDTH, 128), BF16),
            pltpu.VMEM((8, WIDTH), F32),
            pltpu.VMEM((2, EXPERTS, 2, CAP, WIDTH), BF16),
            pltpu.VMEM((2, EXPERTS, 2, CAP, WIDTH), BF16),
            pltpu.VMEM((2, EXPERTS, 2, CAP, WIDTH), BF16),
            pltpu.VMEM((2, EXPERTS, 2, CAP, WIDTH), BF16),
            pltpu.VMEM((tokens, WIDTH), F32),
            pltpu.VMEM((tokens, WIDTH), F32),
            pltpu.VMEM((2, DP, SHARD, WIDTH), BF16),
            pltpu.VMEM((10, 2, half, WIDTH), BF16),
            pltpu.VMEM((10, 2, SHARD, WIDTH), BF16),
            pltpu.VMEM((EXPERTS, WIDTH, main), BF16),
            pltpu.VMEM((2, DP, 4, ROWS, 128), BF16),
            pltpu.VMEM((4, WIDTH, main), BF16),
            pltpu.VMEM((DP, 4, ROWS, 128), BF16),
            pltpu.VMEM((2, WIDTH // 2, main), BF16),
            pltpu.VMEM((2, WIDTH, main), BF16),
            pltpu.VMEM((DP, ROWS, main), BF16),
            pltpu.VMEM((2, 2, 4, ROWS, 128), BF16),
            pltpu.VMEM((2, 4, 4, ROWS, 128), BF16),
            pltpu.VMEM((2, 2, ROWS, 128), BF16),
            pltpu.VMEM((2, 4, ROWS, 128), BF16),
            pltpu.VMEM((4, ROWS, 128), BF16),
            pltpu.VMEM((4, ROWS, 128), BF16),
            pltpu.VMEM((DP, 8, 128), F32),
            pltpu.VMEM((DP, 8, 128), F32),
            pltpu.VMEM((8, 128), F32),
            pltpu.VMEM((EXPERTS, 32, 128), BF16),
            pltpu.VMEM((EXPERTS, 32, 128), BF16),
            pltpu.VMEM((EXPERTS, 8, 128), F32),
            pltpu.VMEM((tokens, WIDTH), BF16),
            pltpu.VMEM((tokens, WIDTH), BF16),
            pltpu.VMEM((tokens, 3 * WIDTH), BF16),
            pltpu.VMEM((HEADS, LEN, LEN), F32),
            pltpu.VMEM((tokens, 128), BF16),
            pltpu.VMEM((8, WIDTH), F32),
            pltpu.VMEM((BUCKETS, HEADS, LEN), F32),
            dma(13),
            dma(5),
            dma(2),
            dma(EXPERTS),
            dma(EXPERTS),
            dma(2, DP),
            dma(2, DP),
            dma(40),
            dma(40),
            dma(10),
            dma(10),
            dma(32),
            dma(32),
            dma(60),
            dma(60),
            dma(11),
            dma(11),
            dma(2, DP),
            dma(2, DP),
            dma(2, EXPERTS),
            dma(2, EXPERTS),
            dma(15),
            dma(15),
        ],
        compiler_params=pltpu.CompilerParams(
            collective_id=0, has_side_effects=True, vmem_limit_bytes=63 * MIB
        ),
        name="layer",
    )(x, cot, ids, slots, buckets, wqkv, wattn, wrouter, row, *small, win, wout)


def hand_over_kernel(*refs):
    n = len(refs) // 3
    sems = refs[-1]
    come = [pltpu.make_async_copy(refs[k], refs[2 * n + k], sems.at[0, k]) for k in range(n)]
    go = [pltpu.make_async_copy(refs[2 * n + k], refs[n + k], sems.at[1, k]) for k in range(n)]
    for copy in come:
        copy.start()
    for k in range(n):
        come[k].wait()
        go[k].start()
    for copy in go:
        copy.wait()


def hand_over(*arrays):
    hbm = pl.BlockSpec(memory_space=pl.ANY)
    return pl.pallas_call(
        hand_over_kernel,
        out_shape=tuple(jax.ShapeDtypeStruct(a.shape, a.dtype) for a in arrays),
        in_specs=[hbm] * len(arrays),
        out_specs=(hbm,) * len(arrays),
        scratch_shapes=[
            *(pltpu.VMEM(a.shape, a.dtype) for a in arrays),
            pltpu.SemaphoreType.DMA((2, len(arrays))),
        ],
        name="hand_over",
    )(*arrays)


def local(
    tokens,
    w_qkv,
    w_attn_out,
    w_router,
    gain_attn,
    gain_moe,
    bias_table,
    w_in,
    w_out,
    expert_ids,
    slots,
    buckets,
    cotangent,
):
    seqs = tokens.shape[0] // LEN
    gap = jnp.zeros((2,), BF16)
    row = jnp.concatenate(
        [jnp.zeros((48,), BF16), gain_attn, gap, gain_moe, gap, bias_table, jnp.zeros((61,), BF16)]
    )
    results = layer(
        tokens,
        cotangent,
        expert_ids.reshape(seqs, LEN),
        slots.reshape(seqs, LEN),
        buckets,
        w_qkv,
        w_attn_out,
        w_router,
        row[None],
        w_in[0],
        w_out[0],
    )
    output, grad_tokens, grad_in, grad_out, grad_qkv, grad_attn, grad_router = hand_over(
        *results[:7]
    )
    small = results[7][0]
    return (
        output,
        grad_tokens,
        grad_qkv,
        grad_attn,
        grad_router,
        small[48:54],
        small[56:62],
        small[64:67],
        grad_in[None],
        grad_out[None],
    )


def solution(mesh):
    spread = ("dp", "expert")
    in_specs = (
        P(spread, None),
        P(spread, None),
        P(spread, None),
        P(spread, None),
        P(spread),
        P(spread),
        P(spread),
        P("expert", "dp", None),
        P("expert", "dp", None),
        P(spread),
        P(spread),
        P(),
        P(spread, None),
    )
    out_specs = (
        P(spread, None),
        P(spread, None),
        P(spread, None),
        P(spread, None),
        P(spread, None),
        P(spread),
        P(spread),
        P(spread),
        P("expert", "dp", None),
        P("expert", "dp", None),
    )
    return jax.shard_map(local, mesh=mesh, in_specs=in_specs, out_specs=out_specs, check_vma=False)
```

```python
import math

import jax
import jax.numpy as jnp
import numpy as np
from jax import lax
from jax.experimental import pallas as pl
from jax.experimental.pallas import tpu as pltpu
from jax.sharding import PartitionSpec as P

MESH = pl.DeviceIdType.MESH
HEADS = 12
HEAD_DIM = 64
BUCKETS = 32
LEN = 128
WIDTH = 768
FF = 3072
EXPERTS = 8
DP = 16
CAP = 16
SHARD = FF // DP
COLS = 384
ROWS = 48
NORM_EPS = 1e-06
HIGH = lax.Precision.HIGHEST
F32 = jnp.float32
BF16 = jnp.bfloat16
MIB = 1 << 20


def place_matrix():
    m = np.zeros((160, 384), np.float32)
    for c in range(3):
        for e in range(8):
            for r in range(6):
                m[c * 48 + e * 6 + r, e * 48 + c * 6 + r] = 1
    for e in range(8):
        m[144 + e, e * 48 + 32] = 1
    return m


def spread_matrix():
    m = np.zeros((256, 144), np.float32)
    for c in range(3):
        for e in range(8):
            for r in range(6):
                m[e * 32 + c * 6 + r, c * 48 + e * 6 + r] = 1
    return m


def small_matrices():
    n = np.arange(WIDTH)
    owner = np.zeros((128, WIDTH), np.float32)
    owner[n // 6, n] = 1
    gains = np.zeros((2, 128, WIDTH), np.float32)
    gains[0, 48 + n % 6, n] = 1
    gains[1, 56 + n % 6, n] = 1
    col = np.arange(128)
    group = ((col[None] // 8 == n[:, None] % 6) & (col[None] < 48)).astype(np.float32)
    fold = np.zeros((128, 128), np.float32)
    fold[np.arange(48), np.arange(48) % 8] = 1
    table = np.zeros((128, 128), np.float32)
    for j in range(4):
        for b in range(BUCKETS):
            table[4 * b + j, j * 32 + b] = 1
    pick = np.zeros((4, 16, 128), np.float32)
    for j in range(4):
        for t in range(3):
            pick[j, 3 * j + t, 64 + t] = 1
    return owner, gains, group, fold, table, pick


class Where:
    def __init__(self):
        self.dp = lax.axis_index("dp")
        self.e = lax.axis_index("expert")
        self.z, self.y = lax.div(self.dp, 4), lax.rem(self.dp, 4)
        self.x, self.c = lax.div(self.e, 2), lax.rem(self.e, 2)
        self.partner_e = self.x * 2 + (1 - self.c)
        self.partner = {"expert": self.partner_e}

    def at(self, axis, step):
        if axis == "y":
            return self.z * 4 + lax.rem(self.y + step + 4, 4)
        if axis == "z":
            return lax.rem(self.z + step + 4, 4) * 4 + self.y
        return lax.rem(self.x + step + 4, 4) * 2 + self.c

    def dev(self, axis, step):
        return {"expert" if axis == "x" else "dp": self.at(axis, step)}

    def at2(self, axis1, step1, step2):
        dy, dz = (step1, step2) if axis1 == "y" else (step2, step1)
        return lax.rem(self.z + dz + 4, 4) * 4 + lax.rem(self.y + dy + 4, 4)


def greet(w):
    barrier = pltpu.get_barrier_semaphore()

    def hello_e(k, n):
        pl.semaphore_signal(
            barrier, inc=1, device_id={"expert": lax.rem(w.e + k, EXPERTS)}, device_id_type=MESH
        )
        return n

    def hello_dp(k, n):
        pl.semaphore_signal(
            barrier, inc=1, device_id={"dp": lax.rem(w.dp + k, DP)}, device_id_type=MESH
        )
        return n

    lax.fori_loop(1, EXPERTS, hello_e, 0)
    lax.fori_loop(1, DP, hello_dp, 0)


def remote(src, dst, send, recv, dev):
    return pltpu.make_async_remote_copy(
        src_ref=src, dst_ref=dst, send_sem=send, recv_sem=recv, device_id=dev, device_id_type=MESH
    )


class FineRingGather:
    def __init__(self, w, axis, place, rows, send, recv):
        self.w, self.axis, self.place, self.half = w, axis, place, rows // 2
        self.send, self.recv = send, recv
        self.copies = []

    def _go(self, step, place, k):
        part = place.at[pl.ds(k * self.half, self.half)]
        n = len(self.copies)
        copy = remote(
            part, part, self.send.at[n], self.recv.at[n], self.w.dev(self.axis, step)
        )
        copy.start()
        self.copies.append(copy)

    def start(self):
        own = self.place(0)
        self._go(1, own, 0)
        self._go(-1, own, 1)
        self._go(1, own, 1)
        self._go(-1, own, 0)

    def relay(self):
        self.copies[0].wait_recv()
        self._go(1, self.place(-1), 0)
        self.copies[1].wait_recv()
        self._go(-1, self.place(1), 1)

    def near(self):
        self.copies[2].wait_recv()
        self.copies[3].wait_recv()

    def finish(self):
        self.copies[4].wait_recv()
        self.copies[5].wait_recv()

    def drain(self):
        for copy in self.copies:
            copy.wait_send()


class RingGather:
    def __init__(self, w, axis, place, rows, send, recv, base, own=None):
        self.w, self.axis, self.place, self.half = w, axis, place, rows // 2
        self.send, self.recv, self.base = send, recv, base
        self.own = place(0) if own is None else own
        self.copies = []

    def _go(self, k, src, dst, step):
        copy = remote(
            src,
            dst,
            self.send.at[self.base + k],
            self.recv.at[self.base + k],
            self.w.dev(self.axis, step),
        )
        copy.start()
        self.copies.append(copy)

    def start(self):
        self._go(0, self.own, self.place(0), 1)
        self._go(1, self.own, self.place(0), -1)

    def relay(self):
        h = self.half
        self.copies[0].wait_recv()
        low = self.place(-1).at[pl.ds(0, h)]
        self._go(2, low, low, 1)
        self.copies[1].wait_recv()
        high = self.place(1).at[pl.ds(h, h)]
        self._go(3, high, high, -1)

    def finish(self):
        self.copies[2].wait_recv()
        self.copies[3].wait_recv()

    def drain(self):
        for copy in self.copies:
            copy.wait_send()


def add_rows(rows, step, dst, *srcs):
    def body(i, n):
        part = pl.ds(pl.multiple_of(i * step, step), step)
        total = srcs[0][part].astype(F32)
        for src in srcs[1:]:
            total = total + src[part].astype(F32)
        dst[part] = total.astype(dst.dtype)
        return n

    lax.fori_loop(0, rows // step, body, 0)


class RingSum:
    def __init__(self, w, axis, place, rows, relayed, landed, send, recv, base):
        self.w, self.axis, self.place, self.rows, self.half = w, axis, place, rows, rows // 2
        self.relayed, self.landed = relayed, landed
        self.send, self.recv, self.base = send, recv, base
        self.copies = {}

    def _go(self, k, src, dst, step):
        copy = remote(
            src,
            dst,
            self.send.at[self.base + k],
            self.recv.at[self.base + k],
            self.w.dev(self.axis, step),
        )
        copy.start()
        self.copies[k] = copy

    def _part(self, ref, k):
        return ref.at[pl.ds(k * self.half, self.half)]

    def far(self):
        self._go(0, self._part(self.place(2), 0), self.relayed.at[0], 1)
        self._go(1, self._part(self.place(2), 1), self.relayed.at[1], -1)

    def near(self):
        self._go(2, self._part(self.place(1), 1), self._part(self.landed.at[0], 1), 1)
        self._go(3, self._part(self.place(-1), 0), self._part(self.landed.at[1], 0), -1)

    def relay(self):
        self.copies[0].wait_recv()
        low = self._part(self.place(1), 0)
        add_rows(self.half, 32, low, low, self.relayed.at[0])
        self._go(4, low, self._part(self.landed.at[0], 0), 1)
        self.copies[1].wait_recv()
        high = self._part(self.place(-1), 1)
        add_rows(self.half, 32, high, high, self.relayed.at[1])
        self._go(5, high, self._part(self.landed.at[1], 1), -1)

    def finish(self, dst):
        for k in (2, 3, 4, 5):
            self.copies[k].wait_recv()
        add_rows(self.rows, 32, dst, self.place(0), self.landed.at[0], self.landed.at[1])

    def drain(self):
        for k in range(6):
            self.copies[k].wait_send()


def contract_last(left, right):
    return lax.dot_general(left, right, (((1,), (1,)), ((), ())), preferred_element_type=F32)


def contract_first(left, right):
    return lax.dot_general(left, right, (((0,), (0,)), ((), ())), preferred_element_type=F32)


def gelu_both(v):
    c = math.sqrt(2.0 / math.pi)
    square = v * v
    t = jnp.tanh(c * v * (1.0 + 0.044715 * square))
    half = 0.5 * (1.0 + t)
    slope = half + 0.5 * v * (1.0 - t * t) * (c * (1.0 + (3.0 * 0.044715) * square))
    return v * half, slope


def exact_dot(left, right):
    return jnp.dot(left, right, precision=HIGH, preferred_element_type=F32)


def layer_kernel(
    x_hbm,
    cot_hbm,
    ids_hbm,
    slots_hbm,
    buckets_hbm,
    wqkv_ref,
    wattn_ref,
    wrouter_ref,
    small_ref,
    place_hbm,
    spread_hbm,
    owner_hbm,
    gains_hbm,
    group_hbm,
    fold_hbm,
    table_hbm,
    pick_hbm,
    win_ref,
    wout_ref,
    output_hbm,
    grad_tokens_hbm,
    in_hbm,
    out_hbm,
    grad_qkv_ref,
    grad_attn_ref,
    router_out_ref,
    gain_one_ref,
    gain_two_ref,
    bias_ref,
    x_ref,
    cot_ref,
    ids_ref,
    slots_ref,
    buckets_ref,
    first_f,
    first_ref,
    place_ref,
    spread_ref,
    owner_ref,
    gains_ref,
    group_ref,
    fold_ref,
    table_ref,
    pick_ref,
    output_ref,
    grad_tokens_ref,
    in_ref,
    out_ref,
    weights,
    dense,
    extra,
    got,
    piece,
    extra_piece,
    qkv,
    attn,
    n1,
    n2,
    h1,
    probs,
    gate,
    p_all,
    bias,
    router,
    gain,
    sent,
    arrived,
    back,
    returned,
    eo,
    dn2e,
    grads,
    relayed,
    landed,
    ddense,
    crossed,
    x_relayed,
    x_landed,
    dp_got,
    dp_extra,
    extra_mine,
    extra_sum,
    last,
    last_got,
    extra_got,
    da,
    dattn,
    dqkv,
    ds_sum,
    dlogits,
    gain_grads,
    bias_rows,
    load_sem,
    store_sem,
    own_sem,
    a2a_send,
    a2a_recv,
    dp_send,
    dp_recv,
    ring_send,
    ring_recv,
    x_send,
    x_recv,
    tok_send,
    tok_recv,
    sum_send,
    sum_recv,
    sx_send,
    sx_recv,
    sdp_send,
    sdp_recv,
    sa_send,
    sa_recv,
):
    w = Where()
    scale = HEAD_DIM ** (-0.5)
    loads = [
        pltpu.make_async_copy(src, dst, load_sem.at[k])
        for k, (src, dst) in enumerate(
            (
                (fold_hbm, fold_ref),
                (place_hbm, place_ref),
                (x_hbm, x_ref),
                (owner_hbm, owner_ref),
                (gains_hbm, gains_ref),
                (group_hbm, group_ref),
                (table_hbm, table_ref),
                (buckets_hbm, buckets_ref),
                (ids_hbm, ids_ref),
                (slots_hbm, slots_ref),
                (cot_hbm, cot_ref),
                (pick_hbm, pick_ref),
                (spread_hbm, spread_ref),
            )
        )
    ]
    for load in loads:
        load.start()
    stores = []

    def store(src, dst):
        copy = pltpu.make_async_copy(src, dst, store_sem.at[len(stores)])
        copy.start()
        stores.append(copy)

    greet(w)
    loads[0].wait()

    first_f[...] = jnp.zeros_like(first_f)
    lane = lax.broadcasted_iota(jnp.int32, (6, 128), 1)
    turn = 8 * lax.broadcasted_iota(jnp.int32, (6, 128), 0)
    routed = contract_last(wrouter_ref[...], fold_ref[:, :EXPERTS])
    routed = jnp.where((lane >= turn) & (lane < turn + 8), routed, 0.0)
    row = jnp.sum(routed, axis=0, keepdims=True) + small_ref[...].astype(F32)
    for e in range(EXPERTS):
        ref, at = (wqkv_ref, e * COLS) if e < 6 else (wattn_ref, (e - 6) * COLS)
        for c in range(3):
            first_f[e, c * 6 : c * 6 + 6] = ref[:, at + c * 128 : at + (c + 1) * 128].astype(F32)
        first_f[e, 32:33] = row
    first_ref[...] = first_f[...].astype(BF16)
    pl.semaphore_wait(pltpu.get_barrier_semaphore(), EXPERTS - 1 + DP - 1)

    def to_expert(k):
        peer = lax.rem(w.e + k, EXPERTS)
        return remote(
            first_ref.at[peer], got.at[w.e], a2a_send.at[k], a2a_recv.at[k], {"expert": peer}
        )

    def start_a2a(k, n):
        to_expert(k).start()
        return n

    lax.fori_loop(1, EXPERTS, start_a2a, 0)
    got[w.e] = first_ref[w.e]
    owns = []
    one, two = {}, {}
    for n, (own, axis1, axis2) in enumerate(((win_ref, "y", "z"), (wout_ref, "z", "y"))):
        keep = pltpu.make_async_copy(own, weights.at[n, w.dp], own_sem.at[n])
        keep.start()
        owns.append(keep)
        one[n] = RingGather(
            w,
            axis1,
            lambda s, n=n, a=axis1: weights.at[n, w.at2(a, s, 0)],
            SHARD,
            ring_send,
            ring_recv,
            n * 20,
            own=own,
        )
        for k, o in enumerate((0, -1, 1, 2)):
            two[n, o] = RingGather(
                w,
                axis2,
                lambda s, n=n, a=axis1, o=o: weights.at[n, w.at2(a, o, s)],
                SHARD,
                ring_send,
                ring_recv,
                n * 20 + 4 + 4 * k,
                own=own if o == 0 else None,
            )
    for n in range(2):
        one[n].start()
    for load in loads[1:]:
        load.wait()

    def end_a2a(k, n):
        copy = to_expert(k)
        copy.wait_recv()
        copy.wait_send()
        return n

    lax.fori_loop(1, EXPERTS, end_a2a, 0)
    placed = jnp.dot(place_ref[...], got[...].reshape(384, 128), preferred_element_type=F32).astype(
        BF16
    )
    for c in range(3):
        piece[:, c * 128 : (c + 1) * 128] = placed[c * 48 : (c + 1) * 48]
    extra_piece[...] = placed[144:160]
    mine = pl.ds(pl.multiple_of(w.dp * ROWS, 16), ROWS)

    def to_dp(k):
        dev = {"dp": lax.rem(w.dp + k, DP)}
        return (
            remote(piece, dense.at[w.e, mine], dp_send.at[0, k], dp_recv.at[0, k], dev),
            remote(extra_piece, extra.at[w.dp], dp_send.at[1, k], dp_recv.at[1, k], dev),
        )

    def start_dp(k, n):
        for copy in to_dp(k):
            copy.start()
        return n

    def end_dp(k, n):
        for copy in to_dp(k):
            copy.wait_recv()
            copy.wait_send()
        return n

    lax.fori_loop(1, DP, start_dp, 0)
    dense[w.e, mine] = piece[...]
    extra[w.dp] = extra_piece[...]
    for n in range(2):
        two[n, 0].start()
    x = x_ref[...].astype(F32)
    rho1 = lax.rsqrt(jnp.mean(x * x, axis=-1, keepdims=True) + NORM_EPS)
    lax.fori_loop(1, DP, end_dp, 0)
    ring = FineRingGather(w, "x", lambda s: dense.at[w.at("x", s)], WIDTH, x_send, x_recv)
    ring.start()

    def across(k, ref):
        copy = remote(ref, ref, x_send.at[6 + k], x_recv.at[6 + k], w.partner)
        copy.start()
        return copy

    pair = [across(0, dense.at[w.e])]
    for n in range(2):
        one[n].relay()
        two[n, -1].start()
        two[n, 1].start()

    small = extra[...].astype(F32)[:, :8].reshape(128, 128).astype(BF16)
    owner = owner_ref[...]
    for n in range(2):
        tiled = jnp.dot(small, gains_ref[n], preferred_element_type=F32)
        gain[n : n + 1] = jnp.sum(tiled * owner.astype(F32), axis=0, keepdims=True)
    rows_small = contract_first(owner, small) * group_ref[...].astype(F32)
    router[...] = jnp.dot(
        rows_small.astype(BF16), fold_ref[...], preferred_element_type=F32
    ).astype(BF16)
    tables = contract_first(small, table_ref[...])
    buckets = buckets_ref[...]
    for h in range(HEADS):
        row = tables[64 + h % 3 : 65 + h % 3]
        bias[h] = jnp.take_along_axis(
            jnp.broadcast_to(row, (LEN, 128)), buckets + 32 * (h // 3), axis=1
        )
    n1[...] = (x * rho1 * gain[0:1]).astype(BF16)

    ring.relay()
    ring.near()
    pair.append(across(1, dense.at[w.at("x", -1)]))
    pair.append(across(2, dense.at[w.at("x", 1)]))
    for n in range(2):
        two[n, 0].relay()
    for n in range(2):
        one[n].finish()
        two[n, 2].start()
    for k in range(2):
        ring.copies[4 + k].wait_recv()
        half = pl.ds(k * (WIDTH // 2), WIDTH // 2)
        pair.append(across(3 + k, dense.at[w.at("x", 2), half]))
    for copy in pair:
        copy.wait_recv()
    for e in range(6):
        qkv[:, e * COLS : (e + 1) * COLS] = jnp.dot(
            n1[...], dense[e], preferred_element_type=F32
        ).astype(BF16)

    low_lanes = lax.broadcasted_iota(jnp.int32, (LEN, 128), 1) < HEAD_DIM
    lanes_of = (low_lanes, jnp.logical_not(low_lanes))
    zero = jnp.zeros((LEN, 128), BF16)

    def lanes_at(block, hp):
        return pl.ds(pl.multiple_of(block * WIDTH + hp * 128, 128), 128)

    def attention(s, lo, hi):
        rows = pl.ds(s * LEN, LEN)

        def pairs(i, n):
            for u in range(2):
                hp = 2 * i + u
                q, k, v = (qkv[rows, lanes_at(b, hp)] for b in range(3))
                outs = []
                for t in range(2):
                    h = 2 * hp + t
                    logit = contract_last(jnp.where(lanes_of[t], q, zero), k) * scale + bias[h]
                    shifted = jnp.exp(logit - jnp.max(logit, axis=-1, keepdims=True))
                    p = shifted / jnp.sum(shifted, axis=-1, keepdims=True)
                    p_all[s * HEADS + h] = p
                    outs.append(jnp.dot(p.astype(BF16), v, preferred_element_type=F32))
                attn[rows, lanes_at(0, hp)] = jnp.where(low_lanes, outs[0], outs[1]).astype(BF16)
            return n

        lax.fori_loop(lo, hi, pairs, 0)

    expert_lane = lax.broadcasted_iota(jnp.int32, (LEN, 128), 1)
    expert_row = lax.broadcasted_iota(jnp.int32, (LEN, 128), 0)
    eye16 = (
        lax.broadcasted_iota(jnp.int32, (16, 128), 0) == lax.broadcasted_iota(jnp.int32, (16, 128), 1)
    ).astype(BF16)

    def routing(s):
        ids, slots = ids_ref[s : s + 1], slots_ref[s : s + 1]
        target = jnp.where(slots < CAP, ids * CAP + slots, -1)
        route = (jnp.broadcast_to(target, (LEN, 128)) == expert_row).astype(F32).astype(BF16)
        hot_t = (
            (jnp.broadcast_to(ids, (16, LEN)) == lax.broadcasted_iota(jnp.int32, (16, LEN), 0))
            .astype(F32)
            .astype(BF16)
        )
        return route, contract_first(hot_t, eye16)

    def second_norm(s):
        rows = pl.ds(s * LEN, LEN)
        for e in range(2):
            cols = pl.ds(e * COLS, COLS)
            h1[rows, cols] = x_ref[rows, cols].astype(F32) + jnp.dot(
                attn[rows], dense[6 + e], preferred_element_type=F32
            )
        h = h1[rows]
        rho2 = lax.rsqrt(jnp.mean(h * h, axis=-1, keepdims=True) + NORM_EPS)
        normed = (h * rho2 * gain[1:2]).astype(BF16)
        n2[rows] = normed
        logits = jnp.dot(normed, router[...], preferred_element_type=F32)
        logits = jnp.where(expert_lane < EXPERTS, logits, -1e30)
        raised = jnp.exp(logits - jnp.max(logits, axis=-1, keepdims=True))
        prob = raised / jnp.sum(raised, axis=-1, keepdims=True)
        route, hot = routing(s)
        g = jnp.sum(prob * hot, axis=-1, keepdims=True)
        probs[rows] = prob
        gate[rows] = jnp.broadcast_to(g, (LEN, 128))
        deo = (g * cot_ref[rows]).astype(BF16)
        for kind, value in enumerate((normed, deo)):
            picked = jnp.dot(route, value, preferred_element_type=F32).astype(BF16)
            for e in range(EXPERTS):
                sent[s, e, kind] = picked[e * CAP : (e + 1) * CAP]

    def token_copy(src, dst, base, s, k):
        peer = lax.rem(w.e + k, EXPERTS)
        at = base + s * EXPERTS + k
        return remote(
            src.at[s, peer], dst.at[s, w.e], tok_send.at[at], tok_recv.at[at], {"expert": peer}
        )

    def send_tokens(src, dst, base, s):
        def begin(k, n):
            token_copy(src, dst, base, s, k).start()
            return n

        lax.fori_loop(1, EXPERTS, begin, 0)
        dst[s, w.e] = src[s, w.e]

    def wait_tokens(src, dst, base, s):
        def end(k, n):
            copy = token_copy(src, dst, base, s, k)
            copy.wait_recv()
            copy.wait_send()
            return n

        lax.fori_loop(1, EXPERTS, end, 0)

    attention(0, 0, 3)
    second_norm(0)
    send_tokens(sent, arrived, 0, 0)
    for n in range(2):
        two[n, -1].relay()
        two[n, 1].relay()
    attention(1, 0, 3)
    second_norm(1)
    send_tokens(sent, arrived, 0, 1)
    for n in range(2):
        two[n, 2].relay()
    for n in range(2):
        for o in (0, -1, 1, 2):
            two[n, o].finish()
    for s in range(2):
        wait_tokens(sent, arrived, 0, s)
    for copy in owns:
        copy.wait()

    axes = (("y", "z"), ("z", "y"))
    order = (2, 1, -1, 0)
    sum1, sum2 = {}, {}
    for n, (axis1, axis2) in enumerate(axes):
        for k, o in enumerate(order):
            sum2[n, o] = RingSum(
                w,
                axis2,
                lambda s, n=n, a=axis1, o=o: grads.at[n, w.at2(a, o, s)],
                SHARD,
                relayed.at[n * 5 + k],
                landed.at[n * 5 + k],
                sum_send,
                sum_recv,
                (n * 5 + k) * 6,
            )
        sum1[n] = RingSum(
            w,
            axis1,
            lambda s, n=n, a=axis1: grads.at[n, w.at2(a, s, 0)],
            SHARD,
            relayed.at[n * 5 + 4],
            landed.at[n * 5 + 4],
            sum_send,
            sum_recv,
            (n * 5 + 4) * 6,
        )
    slots_here = 2 * EXPERTS * CAP
    eo[...] = jnp.zeros_like(eo)
    dn2e[...] = jnp.zeros_like(dn2e)


    def hidden_blocks(one_of, other_of):
        def body(i, n):
            at = [w.at2("y", dy, dz) for dz, dy in (one_of(i), other_of(i))]
            w_in = jnp.concatenate([weights[0, k] for k in at], axis=0)
            w_out = jnp.concatenate([weights[1, k] for k in at], axis=0)
            rows = arrived[:, :, 0].reshape(slots_here, WIDTH)
            drows = arrived[:, :, 1].reshape(slots_here, WIDTH)
            act, slope = gelu_both(contract_last(rows, w_in))
            hid = act.astype(BF16)
            dpre = (contract_last(drows, w_out) * slope).astype(BF16)
            eo[...] += jnp.dot(hid, w_out, preferred_element_type=F32)
            dn2e[...] += jnp.dot(dpre, w_in, preferred_element_type=F32)
            for m, value in enumerate((contract_first(dpre, rows), contract_first(hid, drows))):
                value = value.astype(BF16)
                for k in range(2):
                    grads[m, at[k]] = value[k * SHARD : (k + 1) * SHARD]
            return n

        lax.fori_loop(0, 2, body, 0)

    hidden_blocks(lambda i: (2, 2 * i), lambda i: (2, 2 * i + 1))
    for o in order:
        sum2[0, o].far()
    hidden_blocks(lambda i: (3 * i, 2), lambda i: (1, 2 - 2 * i))
    for o in order:
        sum2[1, o].far()
    hidden_blocks(lambda i: (0, i), lambda i: (3, i))
    hidden_blocks(lambda i: (1, 1 + 2 * i), lambda i: (3 * i, 3))
    for s in (1, 0):
        for e in range(EXPERTS):
            rows = pl.ds((s * EXPERTS + e) * CAP, CAP)
            back[s, e, 0] = eo[rows].astype(BF16)
            back[s, e, 1] = dn2e[rows].astype(BF16)
        send_tokens(back, returned, 16, s)

    for o in order:
        for n in range(2):
            sum2[n, o].near()
    for n in range(2):
        sum2[n, 2].relay()

    gain_grads[...] = jnp.zeros_like(gain_grads)

    def second_norm_back(s):
        rows = pl.ds(s * LEN, LEN)
        route, hot = routing(s)
        combined = contract_first(route, returned[s, :, 0].reshape(LEN, WIDTH))
        g, cot, h = gate[rows, 0:1], cot_ref[rows], h1[rows]
        output_ref[rows] = h + g * combined
        store(output_ref.at[rows], output_hbm.at[rows])
        dgate = jnp.sum(cot * combined, axis=-1, keepdims=True)
        dl = (probs[rows] * (hot - g) * dgate).astype(BF16)
        dlogits[rows] = dl
        dn2 = contract_last(dl, router[...]) + contract_first(
            route, returned[s, :, 1].reshape(LEN, WIDTH)
        )
        rho2 = lax.rsqrt(jnp.mean(h * h, axis=-1, keepdims=True) + NORM_EPS)
        r2 = h * rho2
        gain_grads[1:2] += jnp.sum(dn2 * r2, axis=0, keepdims=True)
        u2 = dn2 * gain[1:2]
        dh1 = cot + rho2 * (u2 - r2 * jnp.mean(u2 * r2, axis=-1, keepdims=True))
        h1[rows] = dh1
        da[rows] = dh1.astype(BF16)
        total = contract_last(da[rows, 0:COLS], dense[6])
        dattn[rows] = (total + contract_last(da[rows, COLS:WIDTH], dense[7])).astype(BF16)

    def attention_back(s, lo, hi):
        rows = pl.ds(s * LEN, LEN)

        def pairs(i, n):
            for u in range(2):
                hp = 2 * i + u
                q, k, v = (qkv[rows, lanes_at(b, hp)] for b in range(3))
                d_out = dattn[rows, lanes_at(0, hp)]
                dqs, dks, dvs = [], [], []
                for t in range(2):
                    h = 2 * hp + t
                    p = p_all[s * HEADS + h]
                    dprob = contract_last(jnp.where(lanes_of[t], d_out, zero), v)
                    ds = p * (dprob - jnp.sum(p * dprob, axis=-1, keepdims=True))
                    if s == 1:
                        ds_sum[h] = ds
                    else:
                        ds_sum[h] += ds
                    ds_b = ds.astype(BF16)
                    dvs.append(contract_first(p.astype(BF16), d_out))
                    dqs.append(jnp.dot(ds_b, k, preferred_element_type=F32))
                    dks.append(contract_first(ds_b, q))
                dqkv[rows, lanes_at(0, hp)] = (
                    jnp.where(low_lanes, dqs[0], dqs[1]) * scale
                ).astype(BF16)
                dqkv[rows, lanes_at(1, hp)] = (
                    jnp.where(low_lanes, dks[0], dks[1]) * scale
                ).astype(BF16)
                dqkv[rows, lanes_at(2, hp)] = jnp.where(low_lanes, dvs[0], dvs[1]).astype(BF16)
            return n

        lax.fori_loop(lo, hi, pairs, 0)

    wait_tokens(back, returned, 16, 1)
    second_norm_back(1)
    for o in (1, -1, 0):
        for n in range(2):
            sum2[n, o].relay()
    attention_back(1, 0, 3)
    wait_tokens(back, returned, 16, 0)
    second_norm_back(0)
    attention_back(0, 0, 3)

    def dense_gradient(e):
        @pl.when(e < 6)
        def _():
            columns = pl.ds(pl.multiple_of(e * COLS, 128), COLS)
            ddense[e] = contract_first(n1[...], dqkv[:, columns]).astype(BF16)

        @pl.when(e >= 6)
        def _():
            columns = pl.ds(pl.multiple_of((e - 6) * COLS, 128), COLS)
            ddense[e] = contract_first(attn[...], da[:, columns]).astype(BF16)

    pair_sum = []
    for k, o in enumerate(order):
        to = lax.rem(w.x + o + 4, 4)
        dense_gradient(2 * to + 1 - w.c)
        copy = remote(
            ddense.at[2 * to + 1 - w.c],
            crossed.at[to],
            sx_send.at[6 + k],
            sx_recv.at[6 + k],
            w.partner,
        )
        copy.start()
        pair_sum.append(copy)
        dense_gradient(2 * to + w.c)

    def add_pair(k):
        pair_sum[k].wait_recv()
        to = lax.rem(w.x + order[k] + 4, 4)
        here = ddense.at[2 * to + w.c]
        add_rows(WIDTH, 32, here, here, crossed.at[to])

    xsum = RingSum(
        w, "x", lambda s: ddense.at[w.at("x", s)], WIDTH, x_relayed, x_landed, sx_send, sx_recv, 0
    )
    add_pair(0)
    xsum.far()
    add_pair(1)
    add_pair(2)
    xsum.near()
    add_pair(3)

    dn1 = contract_last(dqkv[:, 0:COLS], dense[0])
    for e in range(1, 6):
        dn1 = dn1 + contract_last(dqkv[:, e * COLS : (e + 1) * COLS], dense[e])
    x = x_ref[...].astype(F32)
    rho1 = lax.rsqrt(jnp.mean(x * x, axis=-1, keepdims=True) + NORM_EPS)
    r1 = x * rho1
    gain_grads[0:1] = jnp.sum(dn1 * r1, axis=0, keepdims=True)
    u1 = dn1 * gain[0:1]
    grad_tokens_ref[...] = h1[...] + rho1 * (
        u1 - r1 * jnp.mean(u1 * r1, axis=-1, keepdims=True)
    )
    store(grad_tokens_ref, grad_tokens_hbm)
    def bucket(b, n):
        hit = (buckets_ref[...] == b)[None]
        bias_rows[b] = jnp.sum(jnp.where(hit, ds_sum[...], 0.0), axis=1)
        return n

    lax.fori_loop(0, BUCKETS, bucket, 0)
    xsum.relay()
    per_bucket = jnp.sum(bias_rows[...], axis=2)
    per_bucket = jnp.concatenate([per_bucket, jnp.zeros((BUCKETS, 4), F32)], axis=1)
    owner_f = owner_ref[...].astype(F32)
    grad_router = contract_first(n2[...], dlogits[...])
    wide = lax.dot_general(
        grad_router,
        fold_ref[...].astype(F32),
        (((1,), (1,)), ((), ())),
        precision=HIGH,
        preferred_element_type=F32,
    ) * group_ref[...].astype(F32)
    smalls = exact_dot(owner_f, wide)
    for n in range(2):
        smalls = smalls + lax.dot_general(
            owner_f * gain_grads[n : n + 1],
            gains_ref[n].astype(F32),
            (((1,), (1,)), ((), ())),
            precision=HIGH,
            preferred_element_type=F32,
        )
    table = table_ref[...].astype(F32)
    for j in range(4):
        smalls = smalls + exact_dot(
            table[:, j * 32 : (j + 1) * 32], exact_dot(per_bucket, pick_ref[j].astype(F32))
        )
    extra_mine[...] = smalls.reshape(DP, 8, 128)

    def extra_dp(k):
        peer = lax.rem(w.dp + k, DP)
        return remote(
            extra_mine.at[peer],
            dp_extra.at[w.dp],
            sdp_send.at[1, k],
            sdp_recv.at[1, k],
            {"dp": peer},
        )

    def start_extra(k, n):
        extra_dp(k).start()
        return n

    lax.fori_loop(1, DP, start_extra, 0)
    dp_extra[w.dp] = extra_mine[w.dp]
    for n in range(2):
        sum2[n, 2].finish(grads.at[n, w.at2(axes[n][0], 2, 0)])
        sum1[n].far()
    for n in range(2):
        for o in (1, -1):
            sum2[n, o].finish(grads.at[n, w.at2(axes[n][0], o, 0)])
        sum1[n].near()
    xsum.finish(ddense.at[w.e])

    def rows_of(dp):
        return pl.ds(pl.multiple_of(dp * ROWS, 16), ROWS)

    def dense_dp(k):
        peer = lax.rem(w.dp + k, DP)
        return remote(
            ddense.at[w.e, rows_of(peer)],
            dp_got.at[w.dp],
            sdp_send.at[0, k],
            sdp_recv.at[0, k],
            {"dp": peer},
        )

    def start_dense(k, n):
        dense_dp(k).start()
        return n

    def end_dense(k, n):
        for copy in (dense_dp(k), extra_dp(k)):
            copy.wait_recv()
            copy.wait_send()
        return n

    lax.fori_loop(1, DP, start_dense, 0)
    dp_got[w.dp] = ddense[w.e, rows_of(w.dp)]
    for n in range(2):
        sum1[n].relay()
    for n in range(2):
        sum2[n, 0].finish(grads.at[n, w.dp])
    lax.fori_loop(1, DP, end_dense, 0)
    total = dp_got[0].astype(F32)
    extra_total = dp_extra[0]
    for k in range(1, DP):
        total = total + dp_got[k].astype(F32)
        extra_total = extra_total + dp_extra[k]
    extra_sum[...] = extra_total
    flat = jnp.concatenate([total[:, c * 128 : (c + 1) * 128] for c in range(3)], axis=0)
    last[...] = (
        jnp.dot(spread_ref[...], flat.astype(BF16), preferred_element_type=F32)
        .astype(BF16)
        .reshape(EXPERTS, 32, 128)
    )

    def to_owner(k):
        peer = lax.rem(w.e + k, EXPERTS)
        dev = {"expert": peer}
        return (
            remote(last.at[peer], last_got.at[w.e], sa_send.at[0, k], sa_recv.at[0, k], dev),
            remote(extra_sum, extra_got.at[w.e], sa_send.at[1, k], sa_recv.at[1, k], dev),
        )

    def start_owner(k, n):
        for copy in to_owner(k):
            copy.start()
        return n

    def end_owner(k, n):
        for copy in to_owner(k):
            copy.wait_recv()
            copy.wait_send()
        return n

    lax.fori_loop(1, EXPERTS, start_owner, 0)
    last_got[w.e] = last[w.e]
    extra_got[w.e] = extra_sum[...]
    for n, (ref, hbm) in enumerate(((in_ref, in_hbm), (out_ref, out_hbm))):
        sum1[n].finish(ref)
        store(ref, hbm)
    lax.fori_loop(1, EXPERTS, end_owner, 0)
    for e in range(EXPERTS):
        columns = last_got[e].astype(F32)
        ref, at = (grad_qkv_ref, e * COLS) if e < 6 else (grad_attn_ref, (e - 6) * COLS)
        for c in range(3):
            ref[:, at + c * 128 : at + (c + 1) * 128] = columns[c * 6 : c * 6 + 6]
    extra_total = extra_got[0]
    for k in range(1, EXPERTS):
        extra_total = extra_total + extra_got[k]
    extra_sum[...] = extra_total
    row = extra_sum[pl.ds(w.e, 1)]
    gain_one_ref[...] = row[:, 48:54]
    gain_two_ref[...] = row[:, 56:62]
    bias_ref[...] = row[:, 64:67]
    for r in range(6):
        router_out_ref[r : r + 1] = row[:, r * EXPERTS : (r + 1) * EXPERTS]

    for copy in pair:
        copy.wait_send()
    ring.drain()
    for n in range(2):
        one[n].drain()
        for o in (0, -1, 1, 2):
            two[n, o].drain()
    for copy in pair_sum:
        copy.wait_send()
    xsum.drain()
    for copy in stores:
        copy.wait()
    for n in range(2):
        sum1[n].drain()
        for o in order:
            sum2[n, o].drain()


def layer(x, cot, ids, slots, buckets, wqkv, wattn, wrouter, row, win, wout):
    hbm = pl.BlockSpec(memory_space=pl.ANY)
    vmem = pl.BlockSpec(memory_space=pltpu.VMEM)
    tokens = x.shape[0]
    half, main = SHARD // 2, COLS
    small = tuple(jnp.asarray(m, BF16) for m in (place_matrix(), spread_matrix(), *small_matrices()))

    def dma(*shape):
        return pltpu.SemaphoreType.DMA(shape)

    return pl.pallas_call(
        layer_kernel,
        out_shape=(
            jax.ShapeDtypeStruct((tokens, WIDTH), F32),
            jax.ShapeDtypeStruct((tokens, WIDTH), F32),
            jax.ShapeDtypeStruct((SHARD, WIDTH), F32),
            jax.ShapeDtypeStruct((SHARD, WIDTH), F32),
            jax.ShapeDtypeStruct((6, 3 * WIDTH), F32),
            jax.ShapeDtypeStruct((6, WIDTH), F32),
            jax.ShapeDtypeStruct((6, EXPERTS), F32),
            jax.ShapeDtypeStruct((1, 6), F32),
            jax.ShapeDtypeStruct((1, 6), F32),
            jax.ShapeDtypeStruct((1, 3), F32),
        ),
        in_specs=[hbm] * 5 + [vmem] * 4 + [hbm] * 10,
        out_specs=(hbm,) * 4 + (vmem,) * 6,
        scratch_shapes=[
            *(pltpu.VMEM(a.shape, a.dtype) for a in (x, cot, ids, slots, buckets)),
            pltpu.VMEM((EXPERTS, ROWS, 128), F32),
            pltpu.VMEM((EXPERTS, ROWS, 128), BF16),
            *(pltpu.VMEM(a.shape, a.dtype) for a in small),
            pltpu.VMEM((tokens, WIDTH), F32),
            pltpu.VMEM((tokens, WIDTH), F32),
            pltpu.VMEM((SHARD, WIDTH), F32),
            pltpu.VMEM((SHARD, WIDTH), F32),
            pltpu.VMEM((2, DP, SHARD, WIDTH), BF16),
            pltpu.VMEM((EXPERTS, WIDTH, COLS), BF16),
            pltpu.VMEM((DP, 16, 128), BF16),
            pltpu.VMEM((EXPERTS, 48, 128), BF16),
            pltpu.VMEM((ROWS, COLS), BF16),
            pltpu.VMEM((16, 128), BF16),
            pltpu.VMEM((tokens, 3 * WIDTH), BF16),
            pltpu.VMEM((tokens, WIDTH), BF16),
            pltpu.VMEM((tokens, WIDTH), BF16),
            pltpu.VMEM((tokens, WIDTH), BF16),
            pltpu.VMEM((tokens, WIDTH), F32),
            pltpu.VMEM((tokens, 128), F32),
            pltpu.VMEM((tokens, 128), F32),
            pltpu.VMEM((2 * HEADS, LEN, LEN), F32),
            pltpu.VMEM((HEADS, LEN, LEN), F32),
            pltpu.VMEM((WIDTH, 128), BF16),
            pltpu.VMEM((8, WIDTH), F32),
            pltpu.VMEM((2, EXPERTS, 2, CAP, WIDTH), BF16),
            pltpu.VMEM((2, EXPERTS, 2, CAP, WIDTH), BF16),
            pltpu.VMEM((2, EXPERTS, 2, CAP, WIDTH), BF16),
            pltpu.VMEM((2, EXPERTS, 2, CAP, WIDTH), BF16),
            pltpu.VMEM((tokens, WIDTH), F32),
            pltpu.VMEM((tokens, WIDTH), F32),
            pltpu.VMEM((2, DP, SHARD, WIDTH), BF16),
            pltpu.VMEM((10, 2, half, WIDTH), BF16),
            pltpu.VMEM((10, 2, SHARD, WIDTH), BF16),
            pltpu.VMEM((EXPERTS, WIDTH, main), BF16),
            pltpu.VMEM((4, WIDTH, main), BF16),
            pltpu.VMEM((2, WIDTH // 2, main), BF16),
            pltpu.VMEM((2, WIDTH, main), BF16),
            pltpu.VMEM((DP, ROWS, main), BF16),
            pltpu.VMEM((DP, 8, 128), F32),
            pltpu.VMEM((DP, 8, 128), F32),
            pltpu.VMEM((8, 128), F32),
            pltpu.VMEM((EXPERTS, 32, 128), BF16),
            pltpu.VMEM((EXPERTS, 32, 128), BF16),
            pltpu.VMEM((EXPERTS, 8, 128), F32),
            pltpu.VMEM((tokens, WIDTH), BF16),
            pltpu.VMEM((tokens, WIDTH), BF16),
            pltpu.VMEM((tokens, 3 * WIDTH), BF16),
            pltpu.VMEM((HEADS, LEN, LEN), F32),
            pltpu.VMEM((tokens, 128), BF16),
            pltpu.VMEM((8, WIDTH), F32),
            pltpu.VMEM((BUCKETS, HEADS, LEN), F32),
            dma(13),
            dma(5),
            dma(2),
            dma(EXPERTS),
            dma(EXPERTS),
            dma(2, DP),
            dma(2, DP),
            dma(40),
            dma(40),
            dma(11),
            dma(11),
            dma(32),
            dma(32),
            dma(60),
            dma(60),
            dma(11),
            dma(11),
            dma(2, DP),
            dma(2, DP),
            dma(2, EXPERTS),
            dma(2, EXPERTS),
        ],
        compiler_params=pltpu.CompilerParams(
            collective_id=0, has_side_effects=True, vmem_limit_bytes=63 * MIB
        ),
        name="layer",
    )(x, cot, ids, slots, buckets, wqkv, wattn, wrouter, row, *small, win, wout)


def hand_over_kernel(*refs):
    n = len(refs) // 3
    sems = refs[-1]
    come = [pltpu.make_async_copy(refs[k], refs[2 * n + k], sems.at[0, k]) for k in range(n)]
    go = [pltpu.make_async_copy(refs[2 * n + k], refs[n + k], sems.at[1, k]) for k in range(n)]
    for copy in come:
        copy.start()
    for k in range(n):
        come[k].wait()
        go[k].start()
    for copy in go:
        copy.wait()


def hand_over(*arrays):
    hbm = pl.BlockSpec(memory_space=pl.ANY)
    return pl.pallas_call(
        hand_over_kernel,
        out_shape=tuple(jax.ShapeDtypeStruct(a.shape, a.dtype) for a in arrays),
        in_specs=[hbm] * len(arrays),
        out_specs=(hbm,) * len(arrays),
        scratch_shapes=[
            *(pltpu.VMEM(a.shape, a.dtype) for a in arrays),
            pltpu.SemaphoreType.DMA((2, len(arrays))),
        ],
        name="hand_over",
    )(*arrays)


def local(
    tokens,
    w_qkv,
    w_attn_out,
    w_router,
    gain_attn,
    gain_moe,
    bias_table,
    w_in,
    w_out,
    expert_ids,
    slots,
    buckets,
    cotangent,
):
    seqs = tokens.shape[0] // LEN
    gap = jnp.zeros((2,), BF16)
    row = jnp.concatenate(
        [jnp.zeros((48,), BF16), gain_attn, gap, gain_moe, gap, bias_table, jnp.zeros((61,), BF16)]
    )
    results = layer(
        tokens,
        cotangent,
        expert_ids.reshape(seqs, LEN),
        slots.reshape(seqs, LEN),
        buckets,
        w_qkv,
        w_attn_out,
        w_router,
        row[None],
        w_in[0],
        w_out[0],
    )
    results = hand_over(*results)
    output, grad_tokens, grad_in, grad_out, grad_qkv, grad_attn, grad_router = results[:7]
    grad_gain_one, grad_gain_two, grad_bias = (small[0] for small in results[7:])
    return (
        output,
        grad_tokens,
        grad_qkv,
        grad_attn,
        grad_router,
        grad_gain_one,
        grad_gain_two,
        grad_bias,
        grad_in[None],
        grad_out[None],
    )


def solution(mesh):
    spread = ("dp", "expert")
    in_specs = (
        P(spread, None),
        P(spread, None),
        P(spread, None),
        P(spread, None),
        P(spread),
        P(spread),
        P(spread),
        P("expert", "dp", None),
        P("expert", "dp", None),
        P(spread),
        P(spread),
        P(),
        P(spread, None),
    )
    out_specs = (
        P(spread, None),
        P(spread, None),
        P(spread, None),
        P(spread, None),
        P(spread, None),
        P(spread),
        P(spread),
        P(spread),
        P("expert", "dp", None),
        P("expert", "dp", None),
    )
    return jax.shard_map(local, mesh=mesh, in_specs=in_specs, out_specs=out_specs, check_vma=False)
```
